768 devices in a mesh: dp: 24 (over z_lo, x, core), seq: 32 (over y, z_hi).
Axes of the slice: x: 4, y: 8, z: 12 (z_hi: 4, z_lo: 3; z = z_hi * 3 + z_lo), core: 2. Of those that a mesh axis runs over, the one named last changes fastest.
Arguments:
- byte_states: bfloat16 [196608, 1024], P(('dp', 'seq')), parts along dimension 0, may hold values from -20 to 20
- w_qkv: bfloat16 [1024, 3072], replicated
- w_out: bfloat16 [1024, 1024], replicated, may hold values from -0.75 to 0.75
- patch_start: int32 [196608], P(('dp', 'seq')), parts along dimension 0, may hold values from 0 to 1, as said below
- latent_q: bfloat16 [24576, 2048], P(('dp', 'seq')), parts along dimension 0, may hold values from -100 to 100
- latent_k: bfloat16 [24576, 2048], P(('dp', 'seq')), parts along dimension 0, may hold values from -5 to 5
- latent_v: bfloat16 [24576, 2048], P(('dp', 'seq')), parts along dimension 0, may hold values from -6 to 6
Outputs:
- encoded: bfloat16 [196608, 1024], P(('dp', 'seq')), parts along dimension 0
- patch_embed: bfloat16 [24576, 1024], P(('dp', 'seq')), parts along dimension 0
- latent_out: bfloat16 [24576, 2048], P(('dp', 'seq')), parts along dimension 0
The draws below stay inside these ranges and needn't reach their ends.
There are 24 independent parts, one for each index of `dp`. The reference program is written for one: setup_inputs(seed, part) draws one part's arguments, and reference() takes and returns one part's arrays. A program takes and returns all parts, laid end to end along the dimension named above; an argument that names none is the same for every part. Nothing has to cross between parts.
Inputs may be any that keep to these rules, and one draw needn't show every extreme that they name: `patch_start`: byte 0 opens a patch. Each block of 256 bytes holds between 16 and 32 opening bytes, and some block holds exactly 32.
All inputs are finite; a program needn't handle non-finite values.
Results may differ from the reference program's by a relative error of at most 0.007.
Values may be sent and summed in bfloat16 or wider, within the bound.
No kernel may reach another device: no remote copies, remote signals or barrier semaphores. Data moves between devices by JAX's collectives and lax.ppermute only.
A program may use at most 64 MiB of HBM per device.

```python
import math
import jax
import jax.numpy as jnp
from jax import lax

D_BYTE = 1024
BYTE_HEAD = 64
WINDOW = 512
LAT_HEADS = 16
LAT_HEAD = 128
BYTES_DEV = 256
D_LAT = 2048
CAP = 32
BYTES = 8192
SLOTS = 1024
N_SEQ = 32


def draw_byte_states(key, part):
    drawn = jnp.clip(jax.random.normal(key, (BYTES, D_BYTE), jnp.float32), -5.0, 5.0)
    return drawn.astype(jnp.bfloat16)


def draw_w_qkv(key, part):
    drawn = jnp.clip(jax.random.normal(key, (D_BYTE, 3 * D_BYTE), jnp.float32), -5.0, 5.0) / math.sqrt(D_BYTE)
    return drawn.astype(jnp.bfloat16)


def draw_patch_start(key, part):
    count_key, device_key, order_key = jax.random.split(jax.random.fold_in(key, 3), 3)
    blocks = BYTES // BYTES_DEV
    counts = jax.random.randint(count_key, (blocks,), CAP // 2, CAP)
    busiest = jax.random.randint(device_key, (), 1, blocks)
    counts = jnp.where(jnp.arange(blocks) == busiest, CAP, counts)
    order_keys = jax.random.split(order_key, blocks)
    ranks = jax.vmap(lambda single: jax.random.permutation(single, BYTES_DEV))(order_keys)
    start_flags = (ranks < counts[:, None]).astype(jnp.int32)
    start_flags = start_flags.at[0, 0].set(1)
    return start_flags.reshape(BYTES)


def latent_pair(key):
    query_key, keys_key = jax.random.split(jax.random.fold_in(key, 11), 2)
    queries = jnp.clip(jax.random.normal(query_key, (SLOTS, D_LAT), jnp.float32), -5.0, 5.0)
    keys_drawn = jnp.clip(jax.random.normal(keys_key, (SLOTS, D_LAT), jnp.float32), -5.0, 5.0)
    return (queries, keys_drawn)


def draw_latent_q(key, part):
    return latent_pair(key)[0].astype(jnp.bfloat16)


def draw_latent_k(key, part):
    return latent_pair(key)[1].astype(jnp.bfloat16)


def levels(key, extent, pieces, least, largest):
    loudness = 1.0
    for dim, blocks in pieces:
        steps = jax.random.uniform(jax.random.fold_in(jax.random.fold_in(key, 6), dim), (blocks,), jnp.float32, least / len(pieces), largest / len(pieces))
        loudness = loudness * jnp.repeat(jnp.exp(steps), extent[dim] // blocks).reshape((-1,) + (1,) * (len(extent) - 1 - dim))
    return loudness


def bell_draw(stream_key, dims, scale, most, shards=(), kind=jnp.bfloat16):
    values = scale * jax.random.normal(stream_key, dims, jnp.float32)
    if shards:
        values = values * levels(stream_key, dims, shards, -0.22, 0.18)
    return jnp.clip(values, -most, most).astype(kind)


def setup_inputs(seed: int = 0, part: int = 0) -> dict:
    streams_of = jax.random.split(jax.random.key(seed), 8)
    part_keys = jax.random.split(jax.random.fold_in(streams_of[7], part), 8)
    return {
        "byte_states": draw_byte_states(jax.random.fold_in(jax.random.fold_in(streams_of[7], part), 71), part),
        "w_qkv": draw_w_qkv(jax.random.fold_in(streams_of[7], 71), part),
        "w_out": bell_draw(streams_of[2], (D_BYTE, D_BYTE), (D_BYTE // 16) ** -0.5, 0.75),
        "patch_start": draw_patch_start(jax.random.fold_in(jax.random.fold_in(streams_of[7], part), 71), part),
        "latent_q": draw_latent_q(jax.random.fold_in(jax.random.fold_in(streams_of[7], part), 71), part),
        "latent_k": draw_latent_k(jax.random.fold_in(jax.random.fold_in(streams_of[7], part), 71), part),
        "latent_v": bell_draw(part_keys[6], (SLOTS, D_LAT), 1.0, 6.0, ((0, 32),)),
    }


NEGATIVE = -1e30


def attend(query_heads, key_heads, value_heads, visible, head_size):
    scores = jnp.einsum("qhd,khd->hqk", query_heads, key_heads) * (head_size ** -0.5)
    scores = jnp.where(visible[None], scores, NEGATIVE)
    row_peak = jnp.max(scores, axis=-1, keepdims=True)
    weights = jnp.where(visible[None], jnp.exp(scores - row_peak), 0.0)
    normalizer = jnp.sum(weights, axis=-1)
    rounded = lax.optimization_barrier(weights.astype(jnp.bfloat16)).astype(jnp.float32)
    summed = jnp.einsum("hqk,khd->qhd", rounded, value_heads)
    return (summed / jnp.transpose(normalizer)[:, :, None]).astype(jnp.bfloat16)


def byte_block(block_index, queries, padded):
    first_row = block_index * BYTES_DEV
    query_rows = lax.dynamic_slice_in_dim(queries, first_row, BYTES_DEV, 0)
    window_rows = lax.dynamic_slice_in_dim(padded, first_row, BYTES_DEV + WINDOW, 0)
    head_count = D_BYTE // BYTE_HEAD
    query_pos = first_row + jnp.arange(BYTES_DEV, dtype=jnp.int32)
    key_pos = first_row - WINDOW + jnp.arange(BYTES_DEV + WINDOW, dtype=jnp.int32)
    visible = (key_pos[None, :] >= 0) & (key_pos[None, :] <= query_pos[:, None]) & (key_pos[None, :] > query_pos[:, None] - WINDOW)
    query_heads = query_rows.astype(jnp.float32).reshape(BYTES_DEV, head_count, BYTE_HEAD)
    key_heads = window_rows[:, :D_BYTE].astype(jnp.float32).reshape(BYTES_DEV + WINDOW, head_count, BYTE_HEAD)
    value_heads = window_rows[:, D_BYTE:].astype(jnp.float32).reshape(BYTES_DEV + WINDOW, head_count, BYTE_HEAD)
    return attend(query_heads, key_heads, value_heads, visible, BYTE_HEAD).reshape(BYTES_DEV, D_BYTE)


def reference(byte_states, w_qkv, w_out, patch_start, latent_q, latent_k, latent_v):
    projected = jnp.dot(byte_states, w_qkv, preferred_element_type=jnp.float32).astype(jnp.bfloat16)
    queries = projected[:, :D_BYTE]
    padded = jnp.concatenate([jnp.zeros((WINDOW, 2 * D_BYTE), projected.dtype), projected[:, D_BYTE:]], axis=0)
    block_outputs = lax.map(lambda block_index: byte_block(block_index, queries, padded), jnp.arange(N_SEQ, dtype=jnp.int32))
    attended = block_outputs.reshape(BYTES, D_BYTE)
    encoded = (byte_states.astype(jnp.float32) + jnp.dot(attended, w_out, preferred_element_type=jnp.float32)).astype(jnp.bfloat16)

    start_flags = patch_start.reshape(N_SEQ, BYTES_DEV)
    local_rank = (jnp.cumsum(start_flags, axis=1) - 1).astype(jnp.int32)
    device_ids = jnp.arange(N_SEQ, dtype=jnp.int32)[:, None]
    start_slot = jnp.where(start_flags > 0, device_ids * CAP + local_rank, -1).reshape(BYTES).astype(jnp.int32)
    owner_slot = lax.cummax(start_slot, axis=0)
    slot_sums = jax.ops.segment_sum(encoded.astype(jnp.float32), owner_slot, num_segments=SLOTS)
    counts = jax.ops.segment_sum(jnp.ones((BYTES,), jnp.float32), owner_slot, num_segments=SLOTS)
    patch_embed = jnp.where(counts[:, None] > 0, slot_sums / jnp.maximum(counts, 1.0)[:, None], 0.0).astype(jnp.bfloat16)

    per_device = jnp.sum(start_flags, axis=1).astype(jnp.int32)
    slot_index = jnp.arange(SLOTS, dtype=jnp.int32)
    slot_valid = (slot_index % CAP) < per_device[slot_index // CAP]
    visible = (slot_index[None, :] <= slot_index[:, None]) & slot_valid[None, :]
    head_shape = (SLOTS, LAT_HEADS, LAT_HEAD)
    latent_heads = attend(latent_q.astype(jnp.float32).reshape(head_shape), latent_k.astype(jnp.float32).reshape(head_shape), latent_v.astype(jnp.float32).reshape(head_shape), visible, LAT_HEAD)
    latent_out = jnp.where(slot_valid[:, None], latent_heads.reshape(SLOTS, D_LAT), jnp.zeros((), latent_heads.dtype))
    return (encoded, patch_embed, latent_out)
```

```python
import functools

import jax
import jax.numpy as jnp
from jax import lax
from jax.experimental import pallas as pl
from jax.experimental.pallas import tpu as pltpu
from jax.sharding import Mesh, PartitionSpec as P

BYTE_HEAD = 64
LAT_HEAD = 128
GROUP = 256
NEGATIVE = -1e30
MARK = 1024.0
SEQ = ("yh", "yl", "zh")
VMEM_LIMIT = 48 * 1024 * 1024

NT = (((1,), (1,)), ((), ()))


def shift(x, by):
    count = lax.axis_size(SEQ)
    return lax.ppermute(x, SEQ, [(i, i + by) for i in range(count) if 0 <= i + by < count])


def dot(a, b):
    return jnp.dot(a, b, preferred_element_type=jnp.float32)


def dot_nt(a, b):
    return lax.dot_general(a, b, NT, preferred_element_type=jnp.float32)


def params(*semantics):
    if semantics:
        return pltpu.CompilerParams(vmem_limit_bytes=VMEM_LIMIT, dimension_semantics=semantics)
    return pltpu.CompilerParams(vmem_limit_bytes=VMEM_LIMIT)


def pack_kernel(start_ref, q_ref, k_ref, v_ref, out_ref):
    used = jnp.sum(start_ref[...])
    rows = q_ref.shape[0]
    for head in range(out_ref.shape[0]):
        cols = pl.ds(head * LAT_HEAD, LAT_HEAD)
        out_ref[head, 0:rows] = q_ref[:, cols]
        slot = lax.broadcasted_iota(jnp.int32, (rows, LAT_HEAD), 0)
        key = k_ref[:, cols].astype(jnp.float32)
        out_ref[head, rows : 2 * rows] = jnp.where(slot < used, key, MARK).astype(jnp.bfloat16)
        out_ref[head, 2 * rows : 3 * rows] = v_ref[:, cols]


def pack(start_row, q, k, v):
    rows, width = q.shape
    return pl.pallas_call(
        pack_kernel,
        out_shape=jax.ShapeDtypeStruct((width // LAT_HEAD, 3 * rows, LAT_HEAD), jnp.bfloat16),
        compiler_params=params(),
        cost_estimate=pl.CostEstimate(flops=1000, bytes_accessed=6 * rows * width * 2, transcendentals=0),
        name="latent_pack",
    )(start_row, q, k, v)


def latent_kernel(side_ref, own_ref, other_ref, out_ref):
    blocks, rows3, _ = own_ref.shape
    rows = rows3 // 3
    total = blocks * rows
    side = side_ref[0]
    q = own_ref[:, 0:rows].reshape(total, LAT_HEAD)
    scale = LAT_HEAD ** (-0.5)
    pick = (lax.broadcasted_iota(jnp.int32, (16, LAT_HEAD), 1) == 0).astype(jnp.bfloat16)

    def position(index, parity):
        block = index // rows
        return ((block // 4) * 8 + parity * 4 + block % 4) * rows + index % rows

    query_pos = position(lax.broadcasted_iota(jnp.int32, (total, 1), 0), side)
    scores = []
    for which, (ref, parity) in enumerate(((own_ref, side), (other_ref, 1 - side))):
        base = rows if which == 0 else 0
        key = ref[:, base : base + rows].reshape(total, LAT_HEAD)
        mark = dot_nt(pick, key)[0:1]
        key_pos = position(lax.broadcasted_iota(jnp.int32, (1, total), 1), parity)
        key_pos = jnp.where(mark < MARK / 2, key_pos, 1 << 30)
        s = dot_nt(q, key) * scale
        scores.append(jnp.where(key_pos <= query_pos, s, NEGATIVE))
    peak = jnp.maximum(jnp.max(scores[0], axis=1, keepdims=True), jnp.max(scores[1], axis=1, keepdims=True))
    norm = jnp.zeros_like(peak)
    summed = jnp.zeros((total, LAT_HEAD), jnp.float32)
    for which, ref in enumerate((own_ref, other_ref)):
        base = 2 * rows if which == 0 else rows
        value = ref[:, base : base + rows].reshape(total, LAT_HEAD)
        weight = jnp.exp(scores[which] - peak)
        norm = norm + jnp.sum(weight, axis=1, keepdims=True)
        summed = summed + dot(weight.astype(jnp.bfloat16), value)
    out_ref[...] = (summed / norm).astype(jnp.bfloat16).reshape(blocks, rows, LAT_HEAD)


def latent_attend(side, own, other):
    blocks, rows3, width = own.shape
    rows = rows3 // 3
    total = blocks * rows
    return pl.pallas_call(
        latent_kernel,
        out_shape=jax.ShapeDtypeStruct((blocks, rows, width), jnp.bfloat16),
        in_specs=[
            pl.BlockSpec(memory_space=pltpu.SMEM),
            pl.BlockSpec(memory_space=pltpu.VMEM),
            pl.BlockSpec(memory_space=pltpu.VMEM),
        ],
        compiler_params=params(),
        cost_estimate=pl.CostEstimate(
            flops=8 * total * total * width, bytes_accessed=12 * total * width, transcendentals=2 * total * total
        ),
        name="latent_attend",
    )(side, own, other)


def unpack_kernel(start_ref, heads_ref, out_ref):
    used = jnp.sum(start_ref[...])
    rows = out_ref.shape[0]
    for head in range(heads_ref.shape[0]):
        slot = lax.broadcasted_iota(jnp.int32, (rows, LAT_HEAD), 0)
        value = heads_ref[head].astype(jnp.float32)
        out_ref[:, pl.ds(head * LAT_HEAD, LAT_HEAD)] = jnp.where(slot < used, value, 0.0).astype(jnp.bfloat16)


def unpack(start_row, heads):
    count, rows, width = heads.shape
    return pl.pallas_call(
        unpack_kernel,
        out_shape=jax.ShapeDtypeStruct((rows, count * width), jnp.bfloat16),
        compiler_params=params(),
        cost_estimate=pl.CostEstimate(flops=1000, bytes_accessed=4 * count * rows * width, transcendentals=0),
        name="latent_unpack",
    )(start_row, heads)


def in_head(shape, head):
    column = lax.broadcasted_iota(jnp.int32, shape, 1)
    return (column >= head * BYTE_HEAD) & (column < (head + 1) * BYTE_HEAD)


def near_kernel(block_ref, own_ref, before_ref, wq_ref, wk_ref, wv_ref, q_ref, acc_ref, stat_ref):
    rows = own_ref.shape[0]
    own = own_ref[...]
    before = before_ref[...]
    q = dot(own, wq_ref[...]).astype(jnp.bfloat16)
    q = (q.astype(jnp.float32) * BYTE_HEAD ** (-0.5)).astype(jnp.bfloat16)
    q_ref[...] = q
    keys = [dot(x, wk_ref[...]).astype(jnp.bfloat16) for x in (own, before)]
    values = [dot(x, wv_ref[...]).astype(jnp.bfloat16) for x in (own, before)]
    row = lax.broadcasted_iota(jnp.int32, (rows, rows), 0)
    col = lax.broadcasted_iota(jnp.int32, (rows, rows), 1)
    own_seen = col <= row
    before_bias = jnp.where(block_ref[0] >= 1, 0.0, NEGATIVE)
    lane = lax.broadcasted_iota(jnp.int32, (rows, 128), 1)
    acc = jnp.zeros((rows, GROUP), jnp.float32)
    stat = jnp.zeros((rows, 128), jnp.float32)
    heads = GROUP // BYTE_HEAD
    for head in range(heads):
        mask = in_head((rows, GROUP), head)
        qh = jnp.where(mask, q, jnp.zeros_like(q))
        s0 = jnp.where(own_seen, dot_nt(qh, keys[0]), NEGATIVE)
        s1 = dot_nt(qh, keys[1]) + before_bias
        peak = jnp.maximum(jnp.max(s0, axis=1, keepdims=True), jnp.max(s1, axis=1, keepdims=True))
        w0 = jnp.exp(s0 - peak)
        w1 = jnp.exp(s1 - peak)
        norm = jnp.sum(w0, axis=1, keepdims=True) + jnp.sum(w1, axis=1, keepdims=True)
        summed = dot(w0.astype(jnp.bfloat16), values[0]) + dot(w1.astype(jnp.bfloat16), values[1])
        acc = jnp.where(mask, summed, acc)
        stat = jnp.where(lane == head, peak, stat)
        stat = jnp.where(lane == heads + head, norm, stat)
    acc_ref[...] = acc
    stat_ref[...] = stat


def near(block, own, before, w_qkv):
    rows, width = own.shape
    steps = width // GROUP

    def weight(part):
        return pl.BlockSpec((width, GROUP), lambda i: (0, part * steps + i))

    whole = pl.BlockSpec((rows, width), lambda i: (0, 0))
    return pl.pallas_call(
        near_kernel,
        grid=(steps,),
        out_shape=(
            jax.ShapeDtypeStruct((rows, width), jnp.bfloat16),
            jax.ShapeDtypeStruct((rows, width), jnp.float32),
            jax.ShapeDtypeStruct((rows, steps * 128), jnp.float32),
        ),
        in_specs=[pl.BlockSpec(memory_space=pltpu.SMEM), whole, whole, weight(0), weight(1), weight(2)],
        out_specs=(
            pl.BlockSpec((rows, GROUP), lambda i: (0, i)),
            pl.BlockSpec((rows, GROUP), lambda i: (0, i)),
            pl.BlockSpec((rows, 128), lambda i: (0, i)),
        ),
        compiler_params=params("arbitrary"),
        cost_estimate=pl.CostEstimate(
            flops=10 * rows * width * width + 64 * rows * rows * GROUP,
            bytes_accessed=6 * width * width + 8 * rows * width,
            transcendentals=32 * rows * rows,
        ),
        name="near_attention",
    )(block, own, before, w_qkv, w_qkv, w_qkv)


def far_kernel(
    block_ref, start_ref, own_ref, far_ref, q_ref, acc_ref, stat_ref, wk_ref, wv_ref, wo_ref,
    enc_ref, sums_ref, lead_ref, count_ref, total_ref,
):
    step = pl.program_id(0)
    rows = own_ref.shape[0]
    far = far_ref[...]
    key = dot(far, wk_ref[...]).astype(jnp.bfloat16)
    value = dot(far, wv_ref[...]).astype(jnp.bfloat16)
    q = q_ref[...]
    acc = acc_ref[...]
    stat = stat_ref[...]
    row = lax.broadcasted_iota(jnp.int32, (rows, rows), 0)
    col = lax.broadcasted_iota(jnp.int32, (rows, rows), 1)
    first = jnp.where(block_ref[0] >= 2, 0, 2 * rows)
    seen = col > row + first
    heads = GROUP // BYTE_HEAD
    attended = jnp.zeros((rows, GROUP), jnp.float32)
    for head in range(heads):
        mask = in_head((rows, GROUP), head)
        qh = jnp.where(mask, q, jnp.zeros_like(q))
        s = jnp.where(seen, dot_nt(qh, key), NEGATIVE)
        peak = stat[:, head : head + 1]
        norm = stat[:, heads + head : heads + head + 1]
        newer = jnp.maximum(peak, jnp.max(s, axis=1, keepdims=True))
        weight = jnp.exp(s - newer)
        fade = jnp.exp(peak - newer)
        norm = norm * fade + jnp.sum(weight, axis=1, keepdims=True)
        summed = acc * fade + dot(weight.astype(jnp.bfloat16), value)
        attended = jnp.where(mask, summed / norm, attended)
    product = dot(attended.astype(jnp.bfloat16), wo_ref[...])

    @pl.when(step == 0)
    def _():
        total_ref[...] = product

    @pl.when(step > 0)
    def _():
        total_ref[...] += product

    @pl.when(step == pl.num_programs(0) - 1)
    def _():
        encoded = (own_ref[...].astype(jnp.float32) + total_ref[...]).astype(jnp.bfloat16)
        enc_ref[...] = encoded
        slots = sums_ref.shape[0]
        start = jnp.broadcast_to(start_ref[...].astype(jnp.float32), (16, rows)).astype(jnp.bfloat16)
        before_or_at = (row <= col).astype(jnp.float32).astype(jnp.bfloat16)
        rank = dot(start, before_or_at)[0:1].astype(jnp.int32) - 1
        slot = lax.broadcasted_iota(jnp.int32, (slots + 16, rows), 0)
        slot = jnp.where(slot >= slots, slots - 1 - slot, slot)
        onehot = (rank == slot).astype(jnp.float32)
        summed = dot(onehot.astype(jnp.bfloat16), encoded)
        counts = jnp.sum(onehot, axis=1, keepdims=True)
        sums_ref[...] = summed[0:slots]
        count_ref[...] = jnp.broadcast_to(counts[0:slots], (slots, 128))
        width = own_ref.shape[1]
        lead_ref[:, 0:width] = summed[slots : slots + 1]
        lead_ref[:, width : width + 128] = jnp.broadcast_to(counts[slots : slots + 1], (1, 128))


def far_attend(block, start_row, own, far, q, acc, stat, w_qkv, w_out, slots):
    rows, width = own.shape
    steps = width // GROUP

    def weight(part):
        return pl.BlockSpec((width, GROUP), lambda i: (0, part * steps + i))

    def full(shape):
        return pl.BlockSpec(shape, lambda i: (0, 0))

    piece = pl.BlockSpec((rows, GROUP), lambda i: (0, i))
    return pl.pallas_call(
        far_kernel,
        grid=(steps,),
        out_shape=(
            jax.ShapeDtypeStruct((rows, width), jnp.bfloat16),
            jax.ShapeDtypeStruct((slots, width), jnp.float32),
            jax.ShapeDtypeStruct((1, width + 128), jnp.float32),
            jax.ShapeDtypeStruct((slots, 128), jnp.float32),
        ),
        in_specs=[
            pl.BlockSpec(memory_space=pltpu.SMEM),
            full((1, rows)),
            full((rows, width)),
            full((rows, width)),
            piece,
            piece,
            pl.BlockSpec((rows, 128), lambda i: (0, i)),
            weight(1),
            weight(2),
            pl.BlockSpec((GROUP, width), lambda i: (i, 0)),
        ],
        out_specs=(full((rows, width)), full((slots, width)), full((1, width + 128)), full((slots, 128))),
        scratch_shapes=[pltpu.VMEM((rows, width), jnp.float32)],
        compiler_params=params("arbitrary"),
        cost_estimate=pl.CostEstimate(
            flops=6 * rows * width * width + 32 * rows * rows * GROUP,
            bytes_accessed=6 * width * width + 12 * rows * width,
            transcendentals=16 * rows * rows,
        ),
        name="far_attention",
    )(block, start_row, own, far, q, acc, stat, w_qkv, w_qkv, w_out)


def pool_kernel(start_ref, sums_ref, count_ref, extra_ref, out_ref):
    slots, width = sums_ref.shape
    used = jnp.sum(start_ref[...])
    last = lax.broadcasted_iota(jnp.int32, (slots, 1), 0) == used - 1
    extra = extra_ref[...]
    sums = sums_ref[...] + jnp.where(last, extra[:, 0:width], 0.0)
    count = count_ref[:, 0:1] + jnp.where(last, extra[:, width : width + 1], 0.0)
    mean = sums / jnp.maximum(count, 1.0)
    out_ref[...] = jnp.where(count > 0, mean, 0.0).astype(jnp.bfloat16)


def pool(start_row, sums, count, extra):
    return pl.pallas_call(
        pool_kernel,
        out_shape=jax.ShapeDtypeStruct(sums.shape, jnp.bfloat16),
        compiler_params=params(),
        name="patch_pool",
    )(start_row, sums, count, extra)


def local(byte_states, w_qkv, w_out, patch_start, latent_q, latent_k, latent_v):
    rows, _ = byte_states.shape
    slots = latent_q.shape[0]
    block = lax.axis_index(SEQ).astype(jnp.int32).reshape(1)
    side = lax.axis_index("yl").astype(jnp.int32).reshape(1)
    start_row = patch_start.reshape(1, rows)

    before = shift(byte_states, 1)
    far = shift(byte_states, 2)

    packed = pack(start_row, latent_q, latent_k, latent_v)
    own = lax.all_to_all(packed, ("yh", "zh"), 0, 0, tiled=True)
    other = lax.ppermute(own[:, slots:], "yl", [(0, 1), (1, 0)])
    q, acc, stat = near(block, byte_states, before, w_qkv)
    heads = latent_attend(side, own, other)
    returned = lax.all_to_all(heads, ("yh", "zh"), 0, 0, tiled=True)
    latent_out = unpack(start_row, returned)

    encoded, sums, lead, count = far_attend(
        block, start_row, byte_states, far, q, acc, stat, w_qkv, w_out, slots
    )
    extra = shift(lead, -1)
    patch_embed = pool(start_row, sums, count, extra)
    return encoded, patch_embed, latent_out


def solution(mesh):
    folded = Mesh(mesh.devices.reshape(mesh.shape["dp"], 4, 2, 4), ("dp", "yh", "yl", "zh"))
    spec = P(("dp", *SEQ), None)
    return jax.shard_map(
        local,
        mesh=folded,
        in_specs=(spec, P(), P(), P(("dp", *SEQ)), spec, spec, spec),
        out_specs=(spec, spec, spec),
        check_vma=False,
    )
```

```python
import functools

import jax
import jax.numpy as jnp
from jax import lax
from jax.experimental import pallas as pl
from jax.experimental.pallas import tpu as pltpu
from jax.sharding import Mesh, PartitionSpec as P

BYTE_HEAD = 64
LAT_HEAD = 128
GROUP = 256
NEGATIVE = -1e30
UP_ROWS = 128
MARK = 1024.0
SEQ = ("yh", "yl", "zh")
VMEM_LIMIT = 48 * 1024 * 1024

NT = (((1,), (1,)), ((), ()))


def shift(x, by):
    count = lax.axis_size(SEQ)
    return lax.ppermute(x, SEQ, [(i, i + by) for i in range(count) if 0 <= i + by < count])


def down(x, reach):
    count, ring = lax.axis_size(SEQ), lax.axis_size("zh")

    def after(source, steps):
        return source - source % ring + (source - steps) % ring

    sources = range(count - reach)
    for step in range(1, ring - reach):
        x = lax.ppermute(x, SEQ, [(after(s, step - 1), after(s, step)) for s in sources])
    return lax.ppermute(x, SEQ, [(after(s, ring - reach - 1), s + reach) for s in sources])


def dot(a, b):
    return jnp.dot(a, b, preferred_element_type=jnp.float32)


def dot_nt(a, b):
    return lax.dot_general(a, b, NT, preferred_element_type=jnp.float32)


def params(*semantics):
    if semantics:
        return pltpu.CompilerParams(vmem_limit_bytes=VMEM_LIMIT, dimension_semantics=semantics)
    return pltpu.CompilerParams(vmem_limit_bytes=VMEM_LIMIT)


def pack_kernel(start_ref, q_ref, k_ref, v_ref, out_ref):
    used = jnp.sum(start_ref[...])
    rows = q_ref.shape[0]
    for head in range(out_ref.shape[0]):
        cols = pl.ds(head * LAT_HEAD, LAT_HEAD)
        out_ref[head, 0:rows] = q_ref[:, cols]
        slot = lax.broadcasted_iota(jnp.int32, (rows, LAT_HEAD), 0)
        key = k_ref[:, cols].astype(jnp.float32)
        out_ref[head, rows : 2 * rows] = jnp.where(slot < used, key, MARK).astype(jnp.bfloat16)
        out_ref[head, 2 * rows : 3 * rows] = v_ref[:, cols]


def pack(start_row, q, k, v):
    rows, width = q.shape
    return pl.pallas_call(
        pack_kernel,
        out_shape=jax.ShapeDtypeStruct((width // LAT_HEAD, 3 * rows, LAT_HEAD), jnp.bfloat16),
        compiler_params=params(),
        cost_estimate=pl.CostEstimate(flops=1000, bytes_accessed=1000, transcendentals=0),
        name="latent_pack",
    )(start_row, q, k, v)


def latent_kernel(side_ref, own_ref, other_ref, out_ref):
    blocks, rows3, _ = own_ref.shape
    rows = rows3 // 3
    total = blocks * rows
    side = side_ref[0]
    q = own_ref[:, 0:rows].reshape(total, LAT_HEAD)
    scale = LAT_HEAD ** (-0.5)
    pick = (lax.broadcasted_iota(jnp.int32, (16, LAT_HEAD), 1) == 0).astype(jnp.bfloat16)

    def position(index, parity):
        block = index // rows
        return ((block // 4) * 8 + parity * 4 + block % 4) * rows + index % rows

    query_pos = position(lax.broadcasted_iota(jnp.int32, (total, 1), 0), side)
    scores = []
    for which, (ref, parity) in enumerate(((own_ref, side), (other_ref, 1 - side))):
        base = rows if which == 0 else 0
        key = ref[:, base : base + rows].reshape(total, LAT_HEAD)
        mark = dot_nt(pick, key)[0:1]
        key_pos = position(lax.broadcasted_iota(jnp.int32, (1, total), 1), parity)
        key_pos = jnp.where(mark < MARK / 2, key_pos, 1 << 30)
        s = dot_nt(q, key) * scale
        scores.append(jnp.where(key_pos <= query_pos, s, NEGATIVE))
    peak = jnp.maximum(jnp.max(scores[0], axis=1, keepdims=True), jnp.max(scores[1], axis=1, keepdims=True))
    norm = jnp.zeros_like(peak)
    summed = jnp.zeros((total, LAT_HEAD), jnp.float32)
    for which, ref in enumerate((own_ref, other_ref)):
        base = 2 * rows if which == 0 else rows
        value = ref[:, base : base + rows].reshape(total, LAT_HEAD)
        weight = jnp.exp(scores[which] - peak)
        norm = norm + jnp.sum(weight, axis=1, keepdims=True)
        summed = summed + dot(weight.astype(jnp.bfloat16), value)
    out_ref[...] = (summed / norm).astype(jnp.bfloat16).reshape(blocks, rows, LAT_HEAD)


def latent_attend(side, own, other):
    blocks, rows3, width = own.shape
    rows = rows3 // 3
    total = blocks * rows
    return pl.pallas_call(
        latent_kernel,
        out_shape=jax.ShapeDtypeStruct((blocks, rows, width), jnp.bfloat16),
        in_specs=[
            pl.BlockSpec(memory_space=pltpu.SMEM),
            pl.BlockSpec(memory_space=pltpu.VMEM),
            pl.BlockSpec(memory_space=pltpu.VMEM),
        ],
        compiler_params=params(),
        cost_estimate=pl.CostEstimate(flops=1000, bytes_accessed=1000, transcendentals=0),
        name="latent_attend",
    )(side, own, other)


def unpack_kernel(start_ref, heads_ref, out_ref):
    used = jnp.sum(start_ref[...])
    rows = out_ref.shape[0]
    for head in range(heads_ref.shape[0]):
        slot = lax.broadcasted_iota(jnp.int32, (rows, LAT_HEAD), 0)
        value = heads_ref[head].astype(jnp.float32)
        out_ref[:, pl.ds(head * LAT_HEAD, LAT_HEAD)] = jnp.where(slot < used, value, 0.0).astype(jnp.bfloat16)


def unpack(start_row, heads):
    count, rows, width = heads.shape
    return pl.pallas_call(
        unpack_kernel,
        out_shape=jax.ShapeDtypeStruct((rows, count * width), jnp.bfloat16),
        compiler_params=params(),
        cost_estimate=pl.CostEstimate(flops=1000, bytes_accessed=1000, transcendentals=0),
        name="latent_unpack",
    )(start_row, heads)


def halves():
    return [slice(start, start + 128) for start in range(0, GROUP, 128)]


def low_lanes(rows):
    return lax.broadcasted_iota(jnp.int32, (rows, 128), 1) < BYTE_HEAD


def split_heads(x, low, fill):
    other = jnp.full_like(x, fill)
    return jnp.where(low, x, other), jnp.where(low, other, x)


def near_kernel(block_ref, own_ref, before_ref, wq_ref, wk_ref, wv_ref, q_ref, acc_ref, peak_ref, norm_ref):
    rows = own_ref.shape[0]
    own = own_ref[...]
    before = before_ref[...]
    q = dot(own, wq_ref[...]).astype(jnp.bfloat16)
    q = (q.astype(jnp.float32) * BYTE_HEAD ** (-0.5)).astype(jnp.bfloat16)
    q_ref[...] = q
    keys = [dot(x, wk_ref[...]).astype(jnp.bfloat16) for x in (own, before)]
    values = [dot(x, wv_ref[...]).astype(jnp.bfloat16) for x in (own, before)]
    row = lax.broadcasted_iota(jnp.int32, (rows, rows), 0)
    col = lax.broadcasted_iota(jnp.int32, (rows, rows), 1)
    own_seen = col <= row
    before_bias = jnp.where(block_ref[0] >= 1, 0.0, NEGATIVE)
    low = low_lanes(rows)
    for half in halves():
        split_values = [split_heads(v[:, half], low, 1.0) for v in values]
        peaks, products = [], []
        for head, qh in enumerate(split_heads(q[:, half], low, 0.0)):
            s0 = jnp.where(own_seen, dot_nt(qh, keys[0][:, half]), NEGATIVE)
            s1 = dot_nt(qh, keys[1][:, half]) + before_bias
            peak = jnp.max(jnp.maximum(s0, s1), axis=1, keepdims=True)
            w0 = jnp.exp(s0 - peak).astype(jnp.bfloat16)
            w1 = jnp.exp(s1 - peak).astype(jnp.bfloat16)
            peaks.append(peak)
            products.append(dot(w0, split_values[0][head]) + dot(w1, split_values[1][head]))
        acc_ref[:, half] = jnp.where(low, products[0], products[1])
        norm_ref[:, half] = pltpu.roll(jnp.where(low, products[1], products[0]), BYTE_HEAD, 1)
        peak_ref[:, half] = jnp.where(low, peaks[0], peaks[1])


def near(block, own, before, w_qkv):
    rows, width = own.shape
    steps = width // GROUP

    def weight(part):
        return pl.BlockSpec((width, GROUP), lambda i: (0, part * steps + i))

    whole = pl.BlockSpec((rows, width), lambda i: (0, 0))
    return pl.pallas_call(
        near_kernel,
        grid=(steps,),
        out_shape=(
            jax.ShapeDtypeStruct((rows, width), jnp.bfloat16),
            jax.ShapeDtypeStruct((rows, width), jnp.float32),
            jax.ShapeDtypeStruct((rows, width), jnp.float32),
            jax.ShapeDtypeStruct((rows, width), jnp.float32),
        ),
        in_specs=[pl.BlockSpec(memory_space=pltpu.SMEM), whole, whole, weight(0), weight(1), weight(2)],
        out_specs=(pl.BlockSpec((rows, GROUP), lambda i: (0, i)),) * 4,
        compiler_params=params("arbitrary"),
        cost_estimate=pl.CostEstimate(flops=10000000000, bytes_accessed=1000, transcendentals=0),
        name="near_attention",
    )(block, own, before, w_qkv, w_qkv, w_qkv)


def far_kernel(
    block_ref, start_ref, own_ref, up_ref, down_ref, q_ref, acc_ref, peak_ref, norm_ref, wk_ref, wv_ref, wo_ref,
    enc_ref, sums_ref, lead_ref, count_ref, total_ref,
):
    step = pl.program_id(0)
    rows = own_ref.shape[0]
    far = jnp.concatenate([up_ref[...], down_ref[...]], axis=0)
    key = dot(far, wk_ref[...]).astype(jnp.bfloat16)
    value = dot(far, wv_ref[...]).astype(jnp.bfloat16)
    row = lax.broadcasted_iota(jnp.int32, (rows, rows), 0)
    col = lax.broadcasted_iota(jnp.int32, (rows, rows), 1)
    first = jnp.where(block_ref[0] >= 2, 0, 2 * rows)
    seen = col > row + first
    low = low_lanes(rows)
    attended = []
    for half in halves():
        values = split_heads(value[:, half], low, 1.0)
        peak = peak_ref[:, half]
        peaks, products = [], []
        for head, qh in enumerate(split_heads(q_ref[:, half], low, 0.0)):
            s = jnp.where(seen, dot_nt(qh, key[:, half]), NEGATIVE)
            lane = head * BYTE_HEAD
            newer = jnp.maximum(peak[:, lane : lane + 1], jnp.max(s, axis=1, keepdims=True))
            weight = jnp.exp(s - newer).astype(jnp.bfloat16)
            peaks.append(newer)
            products.append(dot(weight, values[head]))
        fade = jnp.exp(peak - jnp.where(low, peaks[0], peaks[1]))
        summed = acc_ref[:, half] * fade + jnp.where(low, products[0], products[1])
        norm = pltpu.roll(jnp.where(low, products[1], products[0]), BYTE_HEAD, 1)
        attended.append((summed / (norm_ref[:, half] * fade + norm)).astype(jnp.bfloat16))
    attended = jnp.concatenate(attended, axis=1)
    product = dot(attended, wo_ref[...])

    @pl.when(step == 0)
    def _():
        total_ref[...] = product

    @pl.when(step > 0)
    def _():
        total_ref[...] += product

    @pl.when(step == pl.num_programs(0) - 1)
    def _():
        encoded = (own_ref[...].astype(jnp.float32) + total_ref[...]).astype(jnp.bfloat16)
        enc_ref[...] = encoded
        slots = sums_ref.shape[0]
        start = jnp.broadcast_to(start_ref[...].astype(jnp.float32), (16, rows)).astype(jnp.bfloat16)
        before_or_at = (row <= col).astype(jnp.float32).astype(jnp.bfloat16)
        rank = dot(start, before_or_at)[0:1].astype(jnp.int32) - 1
        slot = lax.broadcasted_iota(jnp.int32, (slots + 16, rows), 0)
        slot = jnp.where(slot >= slots, slots - 1 - slot, slot)
        onehot = (rank == slot).astype(jnp.float32)
        summed = dot(onehot.astype(jnp.bfloat16), encoded)
        counts = jnp.sum(onehot, axis=1, keepdims=True)
        sums_ref[...] = summed[0:slots]
        count_ref[...] = jnp.broadcast_to(counts[0:slots], (slots, 128))
        width = own_ref.shape[1]
        lead_ref[:, 0:width] = summed[slots : slots + 1]
        lead_ref[:, width : width + 128] = jnp.broadcast_to(counts[slots : slots + 1], (1, 128))


def far_attend(block, start_row, own, far_up, far_down, near_parts, w_qkv, w_out, slots):
    rows, width = own.shape
    steps = width // GROUP

    def weight(part):
        return pl.BlockSpec((width, GROUP), lambda i: (0, part * steps + i))

    def full(shape):
        return pl.BlockSpec(shape, lambda i: (0, 0))

    piece = pl.BlockSpec((rows, GROUP), lambda i: (0, i))
    return pl.pallas_call(
        far_kernel,
        grid=(steps,),
        out_shape=(
            jax.ShapeDtypeStruct((rows, width), jnp.bfloat16),
            jax.ShapeDtypeStruct((slots, width), jnp.float32),
            jax.ShapeDtypeStruct((1, width + 128), jnp.float32),
            jax.ShapeDtypeStruct((slots, 128), jnp.float32),
        ),
        in_specs=[
            pl.BlockSpec(memory_space=pltpu.SMEM),
            full((1, rows)),
            full((rows, width)),
            full(far_up.shape),
            full(far_down.shape),
            piece,
            piece,
            piece,
            piece,
            weight(1),
            weight(2),
            pl.BlockSpec((GROUP, width), lambda i: (i, 0)),
        ],
        out_specs=(full((rows, width)), full((slots, width)), full((1, width + 128)), full((slots, 128))),
        scratch_shapes=[pltpu.VMEM((rows, width), jnp.float32)],
        compiler_params=params("arbitrary"),
        cost_estimate=pl.CostEstimate(flops=20000000000, bytes_accessed=1000, transcendentals=0),
        name="far_attention",
    )(block, start_row, own, far_up, far_down, *near_parts, w_qkv, w_qkv, w_out)


def pool_kernel(start_ref, sums_ref, count_ref, extra_ref, out_ref):
    slots, width = sums_ref.shape
    used = jnp.sum(start_ref[...])
    last = lax.broadcasted_iota(jnp.int32, (slots, 1), 0) == used - 1
    extra = extra_ref[...]
    sums = sums_ref[...] + jnp.where(last, extra[:, 0:width], 0.0)
    count = count_ref[:, 0:1] + jnp.where(last, extra[:, width : width + 1], 0.0)
    mean = sums / jnp.maximum(count, 1.0)
    out_ref[...] = jnp.where(count > 0, mean, 0.0).astype(jnp.bfloat16)


def pool(start_row, sums, count, extra):
    return pl.pallas_call(
        pool_kernel,
        out_shape=jax.ShapeDtypeStruct(sums.shape, jnp.bfloat16),
        compiler_params=params(),
        name="patch_pool",
    )(start_row, sums, count, extra)


def local(byte_states, w_qkv, w_out, patch_start, latent_q, latent_k, latent_v):
    rows, _ = byte_states.shape
    slots = latent_q.shape[0]
    block = lax.axis_index(SEQ).astype(jnp.int32).reshape(1)
    side = lax.axis_index("yl").astype(jnp.int32).reshape(1)
    start_row = patch_start.reshape(1, rows)

    before = shift(byte_states, 1)
    far_down = down(byte_states[UP_ROWS:], 2)
    far_up = shift(before[:UP_ROWS], 1)
    near_parts = near(block, byte_states, before, w_qkv)

    packed = pack(start_row, latent_q, latent_k, latent_v)
    own = lax.all_to_all(packed, ("yh", "zh"), 0, 0, tiled=True)
    other = lax.ppermute(own[:, slots:], "yl", [(0, 1), (1, 0)])
    heads = latent_attend(side, own, other)
    returned = lax.all_to_all(heads, ("yh", "zh"), 0, 0, tiled=True)
    latent_out = unpack(start_row, returned)

    encoded, sums, lead, count = far_attend(
        block, start_row, byte_states, far_up, far_down, near_parts, w_qkv, w_out, slots
    )
    extra = shift(lead, -1)
    patch_embed = pool(start_row, sums, count, extra)
    return encoded, patch_embed, latent_out


def solution(mesh):
    folded = Mesh(mesh.devices.reshape(mesh.shape["dp"], 4, 2, 4), ("dp", "yh", "yl", "zh"))
    spec = P(("dp", *SEQ), None)
    return jax.shard_map(
        local,
        mesh=folded,
        in_specs=(spec, P(), P(), P(("dp", *SEQ)), spec, spec, spec),
        out_specs=(spec, spec, spec),
        check_vma=False,
    )
```

```python
import functools

import jax
import jax.numpy as jnp
from jax import lax
from jax.experimental import pallas as pl
from jax.experimental.pallas import tpu as pltpu
from jax.sharding import Mesh, PartitionSpec as P

BYTE_HEAD = 64
LAT_HEAD = 128
GROUP = 256
NEGATIVE = -1e30
UP_ROWS = 128
MARK = 1024.0
SEQ = ("yh", "yl", "zh")
PACK_COST = 1000
OWN_COST = 30_000_000_000
BEFORE_COST = 10_000_000_000
LATENT_COST = 1000
UNPACK_COST = 1000
FAR_COST = 30_000_000_000
VMEM_ALL = 62 * 1024 * 1024
VMEM_SOME = 16 * 1024 * 1024

NT = (((1,), (1,)), ((), ()))


def shift(x, by):
    count = lax.axis_size(SEQ)
    return lax.ppermute(x, SEQ, [(i, i + by) for i in range(count) if 0 <= i + by < count])


def down(x):
    count, ring = lax.axis_size(SEQ), lax.axis_size("zh")

    def after(source, steps):
        return source - source % ring + (source - steps) % ring

    sources = range(count - 2)
    relayed = lax.ppermute(x, SEQ, [(s, after(s, 1)) for s in sources])
    return relayed, lax.ppermute(relayed, SEQ, [(after(s, 1), s + ring - 2) for s in sources])


def dot(a, b):
    return jnp.dot(a, b, preferred_element_type=jnp.float32)


def dot_nt(a, b):
    return lax.dot_general(a, b, NT, preferred_element_type=jnp.float32)


def params(limit):
    return pltpu.CompilerParams(vmem_limit_bytes=limit)


def pack_kernel(start_ref, q_ref, k_ref, v_ref, out_ref):
    used = jnp.sum(start_ref[...])
    rows = q_ref.shape[0]
    for head in range(out_ref.shape[0]):
        cols = pl.ds(head * LAT_HEAD, LAT_HEAD)
        out_ref[head, 0:rows] = q_ref[:, cols]
        slot = lax.broadcasted_iota(jnp.int32, (rows, LAT_HEAD), 0)
        key = k_ref[:, cols].astype(jnp.float32)
        out_ref[head, rows : 2 * rows] = jnp.where(slot < used, key, MARK).astype(jnp.bfloat16)
        out_ref[head, 2 * rows : 3 * rows] = v_ref[:, cols]


def pack(start_row, q, k, v):
    rows, width = q.shape
    return pl.pallas_call(
        pack_kernel,
        out_shape=jax.ShapeDtypeStruct((width // LAT_HEAD, 3 * rows, LAT_HEAD), jnp.bfloat16),
        compiler_params=params(VMEM_ALL),
        cost_estimate=pl.CostEstimate(flops=PACK_COST, bytes_accessed=1000, transcendentals=0),
        name="latent_pack",
    )(start_row, q, k, v)


def latent_kernel(side_ref, own_ref, other_ref, out_ref):
    blocks, rows3, _ = own_ref.shape
    rows = rows3 // 3
    total = blocks * rows
    side = side_ref[0]
    q = own_ref[:, 0:rows].reshape(total, LAT_HEAD)
    scale = LAT_HEAD ** (-0.5)
    pick = (lax.broadcasted_iota(jnp.int32, (16, LAT_HEAD), 1) == 0).astype(jnp.bfloat16)

    def position(index, parity):
        block = index // rows
        return ((block // 4) * 8 + parity * 4 + block % 4) * rows + index % rows

    query_pos = position(lax.broadcasted_iota(jnp.int32, (total, 1), 0), side)
    scores = []
    for which, (ref, parity) in enumerate(((own_ref, side), (other_ref, 1 - side))):
        base = rows if which == 0 else 0
        key = ref[:, base : base + rows].reshape(total, LAT_HEAD)
        mark = dot_nt(pick, key)[0:1]
        key_pos = position(lax.broadcasted_iota(jnp.int32, (1, total), 1), parity)
        key_pos = jnp.where(mark < MARK / 2, key_pos, 1 << 30)
        s = dot_nt(q, key) * scale
        scores.append(jnp.where(key_pos <= query_pos, s, NEGATIVE))
    peak = jnp.maximum(jnp.max(scores[0], axis=1, keepdims=True), jnp.max(scores[1], axis=1, keepdims=True))
    norm = jnp.zeros_like(peak)
    summed = jnp.zeros((total, LAT_HEAD), jnp.float32)
    for which, ref in enumerate((own_ref, other_ref)):
        base = 2 * rows if which == 0 else rows
        value = ref[:, base : base + rows].reshape(total, LAT_HEAD)
        weight = jnp.exp(scores[which] - peak)
        norm = norm + jnp.sum(weight, axis=1, keepdims=True)
        summed = summed + dot(weight.astype(jnp.bfloat16), value)
    out_ref[...] = (summed / norm).astype(jnp.bfloat16).reshape(blocks, rows, LAT_HEAD)


def latent_attend(side, own, other):
    blocks, rows3, width = own.shape
    rows = rows3 // 3
    total = blocks * rows
    return pl.pallas_call(
        latent_kernel,
        out_shape=jax.ShapeDtypeStruct((blocks, rows, width), jnp.bfloat16),
        in_specs=[
            pl.BlockSpec(memory_space=pltpu.SMEM),
            pl.BlockSpec(memory_space=pltpu.VMEM),
            pl.BlockSpec(memory_space=pltpu.VMEM),
        ],
        compiler_params=params(VMEM_SOME),
        cost_estimate=pl.CostEstimate(flops=LATENT_COST, bytes_accessed=1000, transcendentals=0),
        name="latent_attend",
    )(side, own, other)


def unpack_kernel(start_ref, heads_ref, out_ref):
    used = jnp.sum(start_ref[...])
    rows = out_ref.shape[0]
    for head in range(heads_ref.shape[0]):
        slot = lax.broadcasted_iota(jnp.int32, (rows, LAT_HEAD), 0)
        value = heads_ref[head].astype(jnp.float32)
        out_ref[:, pl.ds(head * LAT_HEAD, LAT_HEAD)] = jnp.where(slot < used, value, 0.0).astype(jnp.bfloat16)


def unpack(start_row, heads):
    count, rows, width = heads.shape
    return pl.pallas_call(
        unpack_kernel,
        out_shape=jax.ShapeDtypeStruct((rows, count * width), jnp.bfloat16),
        compiler_params=params(VMEM_SOME),
        cost_estimate=pl.CostEstimate(flops=UNPACK_COST, bytes_accessed=1000, transcendentals=0),
        name="latent_unpack",
    )(start_row, heads)


def halves():
    return [slice(start, start + 128) for start in range(0, GROUP, 128)]


def low_lanes(rows):
    return lax.broadcasted_iota(jnp.int32, (rows, 128), 1) < BYTE_HEAD


def split_heads(x, low, fill):
    other = jnp.full_like(x, fill)
    return jnp.where(low, x, other), jnp.where(low, other, x)


def own_kernel(own_ref, wq_ref, wk_ref, wv_ref, q_ref, acc_ref, peak_ref, norm_ref):
    rows = own_ref.shape[0]
    own = own_ref[...]
    q = dot(own, wq_ref[...]).astype(jnp.bfloat16)
    q = (q.astype(jnp.float32) * BYTE_HEAD ** (-0.5)).astype(jnp.bfloat16)
    q_ref[...] = q
    key = dot(own, wk_ref[...]).astype(jnp.bfloat16)
    value = dot(own, wv_ref[...]).astype(jnp.bfloat16)
    row = lax.broadcasted_iota(jnp.int32, (rows, rows), 0)
    col = lax.broadcasted_iota(jnp.int32, (rows, rows), 1)
    seen = col <= row
    low = low_lanes(rows)
    for half in halves():
        values = split_heads(value[:, half], low, 1.0)
        peaks, products = [], []
        for head, qh in enumerate(split_heads(q[:, half], low, 0.0)):
            s = jnp.where(seen, dot_nt(qh, key[:, half]), NEGATIVE)
            peak = jnp.max(s, axis=1, keepdims=True)
            peaks.append(peak)
            products.append(dot(jnp.exp(s - peak).astype(jnp.bfloat16), values[head]))
        acc_ref[:, half] = jnp.where(low, products[0], products[1])
        norm_ref[:, half] = pltpu.roll(jnp.where(low, products[1], products[0]), BYTE_HEAD, 1)
        peak_ref[:, half] = jnp.where(low, peaks[0], peaks[1])


def earlier_block(x, half, q_ref, acc_ref, peak_ref, norm_ref, key, value, seen):
    low = low_lanes(x)
    values = split_heads(value[:, half], low, 1.0)
    peak = peak_ref[:, half]
    peaks, products = [], []
    for head, qh in enumerate(split_heads(q_ref[:, half], low, 0.0)):
        s = jnp.where(seen, dot_nt(qh, key[:, half]), NEGATIVE)
        lane = head * BYTE_HEAD
        newer = jnp.maximum(peak[:, lane : lane + 1], jnp.max(s, axis=1, keepdims=True))
        peaks.append(newer)
        products.append(dot(jnp.exp(s - newer).astype(jnp.bfloat16), values[head]))
    newest = jnp.where(low, peaks[0], peaks[1])
    fade = jnp.exp(peak - newest)
    acc = acc_ref[:, half] * fade + jnp.where(low, products[0], products[1])
    norm = pltpu.roll(jnp.where(low, products[1], products[0]), BYTE_HEAD, 1)
    return acc, newest, norm_ref[:, half] * fade + norm


def before_kernel(
    block_ref, before_ref, q_ref, acc_ref, peak_ref, norm_ref, wk_ref, wv_ref, acc_out, peak_out, norm_out
):
    rows = before_ref.shape[0]
    before = before_ref[...]
    key = dot(before, wk_ref[...]).astype(jnp.bfloat16)
    value = dot(before, wv_ref[...]).astype(jnp.bfloat16)
    first = jnp.where(block_ref[0] >= 1, 0, rows)
    seen = lax.broadcasted_iota(jnp.int32, (rows, rows), 1) >= first
    for half in halves():
        acc, peak, norm = earlier_block(rows, half, q_ref, acc_ref, peak_ref, norm_ref, key, value, seen)
        acc_out[:, half] = acc
        peak_out[:, half] = peak
        norm_out[:, half] = norm


def weight_part(width, part):
    steps = width // GROUP
    return pl.BlockSpec((width, GROUP), lambda i: (0, part * steps + i))


def own_attend(own, w_qkv):
    rows, width = own.shape
    piece = pl.BlockSpec((rows, GROUP), lambda i: (0, i))
    kept = jax.ShapeDtypeStruct((rows, width), jnp.float32)
    return pl.pallas_call(
        own_kernel,
        grid=(width // GROUP,),
        out_shape=(jax.ShapeDtypeStruct((rows, width), jnp.bfloat16), kept, kept, kept),
        in_specs=[pl.BlockSpec((rows, width), lambda i: (0, 0))] + [weight_part(width, part) for part in range(3)],
        out_specs=(piece,) * 4,
        compiler_params=params(VMEM_ALL),
        cost_estimate=pl.CostEstimate(flops=OWN_COST, bytes_accessed=1000, transcendentals=0),
        name="own_attention",
    )(own, w_qkv, w_qkv, w_qkv)


def before_attend(block, before, parts, w_qkv):
    rows, width = before.shape
    piece = pl.BlockSpec((rows, GROUP), lambda i: (0, i))
    kept = jax.ShapeDtypeStruct((rows, width), jnp.float32)
    return pl.pallas_call(
        before_kernel,
        grid=(width // GROUP,),
        out_shape=(kept, kept, kept),
        in_specs=[pl.BlockSpec(memory_space=pltpu.SMEM), pl.BlockSpec((rows, width), lambda i: (0, 0))]
        + [piece] * 4
        + [weight_part(width, part) for part in (1, 2)],
        out_specs=(piece,) * 3,
        compiler_params=params(VMEM_ALL),
        cost_estimate=pl.CostEstimate(flops=BEFORE_COST, bytes_accessed=1000, transcendentals=0),
        name="before_attention",
    )(block, before, *parts, w_qkv, w_qkv)


def far_kernel(
    block_ref, start_ref, own_ref, up_ref, down_ref, q_ref, acc_ref, peak_ref, norm_ref, wk_ref, wv_ref, wo_ref,
    enc_ref, sums_ref, lead_ref, count_ref, total_ref,
):
    step = pl.program_id(0)
    rows = own_ref.shape[0]
    far = jnp.concatenate([up_ref[...], down_ref[...]], axis=0)
    key = dot(far, wk_ref[...]).astype(jnp.bfloat16)
    value = dot(far, wv_ref[...]).astype(jnp.bfloat16)
    row = lax.broadcasted_iota(jnp.int32, (rows, rows), 0)
    col = lax.broadcasted_iota(jnp.int32, (rows, rows), 1)
    first = jnp.where(block_ref[0] >= 2, 0, 2 * rows)
    seen = col > row + first
    attended = []
    for half in halves():
        acc, _, norm = earlier_block(rows, half, q_ref, acc_ref, peak_ref, norm_ref, key, value, seen)
        attended.append((acc / norm).astype(jnp.bfloat16))
    attended = jnp.concatenate(attended, axis=1)
    product = dot(attended, wo_ref[...])

    @pl.when(step == 0)
    def _():
        total_ref[...] = product

    @pl.when(step > 0)
    def _():
        total_ref[...] += product

    @pl.when(step == pl.num_programs(0) - 1)
    def _():
        encoded = (own_ref[...].astype(jnp.float32) + total_ref[...]).astype(jnp.bfloat16)
        enc_ref[...] = encoded
        slots = sums_ref.shape[0]
        start = jnp.broadcast_to(start_ref[...].astype(jnp.float32), (16, rows)).astype(jnp.bfloat16)
        before_or_at = (row <= col).astype(jnp.float32).astype(jnp.bfloat16)
        rank = dot(start, before_or_at)[0:1].astype(jnp.int32) - 1
        slot = lax.broadcasted_iota(jnp.int32, (slots + 16, rows), 0)
        slot = jnp.where(slot >= slots, slots - 1 - slot, slot)
        onehot = (rank == slot).astype(jnp.float32)
        summed = dot(onehot.astype(jnp.bfloat16), encoded)
        counts = jnp.sum(onehot, axis=1, keepdims=True)
        sums_ref[...] = summed[0:slots]
        count_ref[...] = jnp.broadcast_to(counts[0:slots], (slots, 128))
        width = own_ref.shape[1]
        lead_ref[:, 0:width] = summed[slots : slots + 1]
        lead_ref[:, width : width + 128] = jnp.broadcast_to(counts[slots : slots + 1], (1, 128))


def far_attend(block, start_row, own, far_up, far_down, parts, w_qkv, w_out, slots):
    rows, width = own.shape
    steps = width // GROUP

    def weight(part):
        return pl.BlockSpec((width, GROUP), lambda i: (0, part * steps + i))

    def full(shape):
        return pl.BlockSpec(shape, lambda i: (0, 0))

    piece = pl.BlockSpec((rows, GROUP), lambda i: (0, i))
    return pl.pallas_call(
        far_kernel,
        grid=(steps,),
        out_shape=(
            jax.ShapeDtypeStruct((rows, width), jnp.bfloat16),
            jax.ShapeDtypeStruct((slots, width), jnp.float32),
            jax.ShapeDtypeStruct((1, width + 128), jnp.float32),
            jax.ShapeDtypeStruct((slots, 128), jnp.float32),
        ),
        in_specs=[
            pl.BlockSpec(memory_space=pltpu.SMEM),
            full((1, rows)),
            full((rows, width)),
            full(far_up.shape),
            full(far_down.shape),
            piece,
            piece,
            piece,
            piece,
            weight(1),
            weight(2),
            pl.BlockSpec((GROUP, width), lambda i: (i, 0)),
        ],
        out_specs=(full((rows, width)), full((slots, width)), full((1, width + 128)), full((slots, 128))),
        scratch_shapes=[pltpu.VMEM((rows, width), jnp.float32)],
        compiler_params=params(VMEM_ALL),
        cost_estimate=pl.CostEstimate(flops=FAR_COST, bytes_accessed=1000, transcendentals=0),
        name="far_attention",
    )(block, start_row, own, far_up, far_down, *parts, w_qkv, w_qkv, w_out)


def pool_kernel(start_ref, sums_ref, count_ref, extra_ref, out_ref):
    slots, width = sums_ref.shape
    used = jnp.sum(start_ref[...])
    last = lax.broadcasted_iota(jnp.int32, (slots, 1), 0) == used - 1
    extra = extra_ref[...]
    sums = sums_ref[...] + jnp.where(last, extra[:, 0:width], 0.0)
    count = count_ref[:, 0:1] + jnp.where(last, extra[:, width : width + 1], 0.0)
    mean = sums / jnp.maximum(count, 1.0)
    out_ref[...] = jnp.where(count > 0, mean, 0.0).astype(jnp.bfloat16)


def pool(start_row, sums, count, extra):
    return pl.pallas_call(
        pool_kernel,
        out_shape=jax.ShapeDtypeStruct(sums.shape, jnp.bfloat16),
        compiler_params=params(VMEM_SOME),
        name="patch_pool",
    )(start_row, sums, count, extra)


def local(byte_states, w_qkv, w_out, patch_start, latent_q, latent_k, latent_v):
    rows, _ = byte_states.shape
    slots = latent_q.shape[0]
    block = lax.axis_index(SEQ).astype(jnp.int32).reshape(1)
    side = lax.axis_index("yl").astype(jnp.int32).reshape(1)
    start_row = patch_start.reshape(1, rows)

    before = shift(byte_states, 1)
    relayed, far_down = down(byte_states[UP_ROWS:])
    far_up = shift(before[:UP_ROWS], 1)
    query, *parts = own_attend(byte_states, w_qkv)
    parts = before_attend(block, before, (query, *parts), w_qkv)

    packed = pack(start_row, latent_q, latent_k, latent_v)
    own = lax.all_to_all(packed, ("yh", "zh"), 0, 0, tiled=True)
    other = lax.ppermute(own[:, slots:], "yl", [(0, 1), (1, 0)])
    heads = latent_attend(side, own, other)
    returned = lax.all_to_all(heads, ("yh", "zh"), 0, 0, tiled=True)
    latent_out = unpack(start_row, returned)

    encoded, sums, lead, count = far_attend(
        block, start_row, byte_states, far_up, far_down, (query, *parts), w_qkv, w_out, slots
    )
    extra = shift(lead, -1)
    patch_embed = pool(start_row, sums, count, extra)
    return encoded, patch_embed, latent_out


def solution(mesh):
    folded = Mesh(mesh.devices.reshape(mesh.shape["dp"], 4, 2, 4), ("dp", "yh", "yl", "zh"))
    spec = P(("dp", *SEQ), None)
    return jax.shard_map(
        local,
        mesh=folded,
        in_specs=(spec, P(), P(), P(("dp", *SEQ)), spec, spec, spec),
        out_specs=(spec, spec, spec),
        check_vma=False,
    )
```

```python
import functools

import jax
import jax.numpy as jnp
from jax import lax
from jax.experimental import pallas as pl
from jax.experimental.pallas import tpu as pltpu
from jax.sharding import Mesh, PartitionSpec as P

BYTE_HEAD = 64
LAT_HEAD = 128
GROUP = 256
NEGATIVE = -1e30
UP_ROWS = 96
MARK = 1024.0
SEQ = ("yh", "yl", "zh")
PACK_COST = 1000
OWN_COST = 30_000_000_000
BEFORE_COST = 10_000_000_000
LATENT_COST = 1000
UNPACK_COST = 1000
FAR_COST = 30_000_000_000
VMEM_ALL = 62 * 1024 * 1024
VMEM_SOME = 16 * 1024 * 1024

NT = (((1,), (1,)), ((), ()))


def shift(x, by):
    count = lax.axis_size(SEQ)
    return lax.ppermute(x, SEQ, [(i, i + by) for i in range(count) if 0 <= i + by < count])


def down(x):
    count, ring = lax.axis_size(SEQ), lax.axis_size("zh")

    def after(source, steps):
        return source - source % ring + (source - steps) % ring

    sources = range(count - 2)
    relayed = lax.ppermute(x, SEQ, [(s, after(s, 1)) for s in sources])
    return relayed, lax.ppermute(relayed, SEQ, [(after(s, 1), s + ring - 2) for s in sources])


def dot(a, b):
    return jnp.dot(a, b, preferred_element_type=jnp.float32)


def dot_nt(a, b):
    return lax.dot_general(a, b, NT, preferred_element_type=jnp.float32)


def params(limit):
    return pltpu.CompilerParams(vmem_limit_bytes=limit)


def pack_kernel(start_ref, q_ref, k_ref, v_ref, out_ref):
    used = jnp.sum(start_ref[...])
    rows = q_ref.shape[0]
    for head in range(out_ref.shape[0]):
        cols = pl.ds(head * LAT_HEAD, LAT_HEAD)
        out_ref[head, 0:rows] = q_ref[:, cols]
        slot = lax.broadcasted_iota(jnp.int32, (rows, LAT_HEAD), 0)
        key = k_ref[:, cols].astype(jnp.float32)
        out_ref[head, rows : 2 * rows] = jnp.where(slot < used, key, MARK).astype(jnp.bfloat16)
        out_ref[head, 2 * rows : 3 * rows] = v_ref[:, cols]


def pack(start_row, q, k, v):
    rows, width = q.shape
    return pl.pallas_call(
        pack_kernel,
        out_shape=jax.ShapeDtypeStruct((width // LAT_HEAD, 3 * rows, LAT_HEAD), jnp.bfloat16),
        compiler_params=params(VMEM_ALL),
        cost_estimate=pl.CostEstimate(flops=PACK_COST, bytes_accessed=1000, transcendentals=0),
        name="latent_pack",
    )(start_row, q, k, v)


def latent_kernel(side_ref, own_ref, other_ref, out_ref):
    blocks, rows3, _ = own_ref.shape
    rows = rows3 // 3
    total = blocks * rows
    side = side_ref[0]
    q = own_ref[:, 0:rows].reshape(total, LAT_HEAD)
    scale = LAT_HEAD ** (-0.5)
    pick = (lax.broadcasted_iota(jnp.int32, (16, LAT_HEAD), 1) == 0).astype(jnp.bfloat16)

    def position(index, parity):
        block = index // rows
        return ((block // 4) * 8 + parity * 4 + block % 4) * rows + index % rows

    query_pos = position(lax.broadcasted_iota(jnp.int32, (total, 1), 0), side)
    scores = []
    for which, (ref, parity) in enumerate(((own_ref, side), (other_ref, 1 - side))):
        base = rows if which == 0 else 0
        key = ref[:, base : base + rows].reshape(total, LAT_HEAD)
        mark = dot_nt(pick, key)[0:1]
        key_pos = position(lax.broadcasted_iota(jnp.int32, (1, total), 1), parity)
        key_pos = jnp.where(mark < MARK / 2, key_pos, 1 << 30)
        s = dot_nt(q, key) * scale
        scores.append(jnp.where(key_pos <= query_pos, s, NEGATIVE))
    peak = jnp.maximum(jnp.max(scores[0], axis=1, keepdims=True), jnp.max(scores[1], axis=1, keepdims=True))
    norm = jnp.zeros_like(peak)
    summed = jnp.zeros((total, LAT_HEAD), jnp.float32)
    for which, ref in enumerate((own_ref, other_ref)):
        base = 2 * rows if which == 0 else rows
        value = ref[:, base : base + rows].reshape(total, LAT_HEAD)
        weight = jnp.exp(scores[which] - peak)
        norm = norm + jnp.sum(weight, axis=1, keepdims=True)
        summed = summed + dot(weight.astype(jnp.bfloat16), value)
    out_ref[...] = (summed / norm).astype(jnp.bfloat16).reshape(blocks, rows, LAT_HEAD)


def latent_attend(side, own, other):
    blocks, rows3, width = own.shape
    rows = rows3 // 3
    total = blocks * rows
    return pl.pallas_call(
        latent_kernel,
        out_shape=jax.ShapeDtypeStruct((blocks, rows, width), jnp.bfloat16),
        in_specs=[
            pl.BlockSpec(memory_space=pltpu.SMEM),
            pl.BlockSpec(memory_space=pltpu.VMEM),
            pl.BlockSpec(memory_space=pltpu.VMEM),
        ],
        compiler_params=params(VMEM_SOME),
        cost_estimate=pl.CostEstimate(flops=LATENT_COST, bytes_accessed=1000, transcendentals=0),
        name="latent_attend",
    )(side, own, other)


def split_kernel(own_ref, after_ref, out_ref):
    del after_ref
    rows = out_ref.shape[1] // 2
    out_ref[...] = own_ref[:, rows : 3 * rows]


def split(own, after):
    blocks, rows3, width = own.shape
    return pl.pallas_call(
        split_kernel,
        out_shape=jax.ShapeDtypeStruct((blocks, rows3 // 3 * 2, width), jnp.bfloat16),
        in_specs=[pl.BlockSpec(memory_space=pltpu.VMEM), pl.BlockSpec(memory_space=pl.ANY)],
        compiler_params=params(VMEM_SOME),
        cost_estimate=pl.CostEstimate(flops=1000, bytes_accessed=1000, transcendentals=0),
        name="latent_split",
    )(own, after)


def unpack_kernel(start_ref, heads_ref, out_ref):
    used = jnp.sum(start_ref[...])
    rows = out_ref.shape[0]
    for head in range(heads_ref.shape[0]):
        slot = lax.broadcasted_iota(jnp.int32, (rows, LAT_HEAD), 0)
        value = heads_ref[head].astype(jnp.float32)
        out_ref[:, pl.ds(head * LAT_HEAD, LAT_HEAD)] = jnp.where(slot < used, value, 0.0).astype(jnp.bfloat16)


def unpack(start_row, heads):
    count, rows, width = heads.shape
    return pl.pallas_call(
        unpack_kernel,
        out_shape=jax.ShapeDtypeStruct((rows, count * width), jnp.bfloat16),
        compiler_params=params(VMEM_SOME),
        cost_estimate=pl.CostEstimate(flops=UNPACK_COST, bytes_accessed=1000, transcendentals=0),
        name="latent_unpack",
    )(start_row, heads)


def halves():
    return [slice(start, start + 128) for start in range(0, GROUP, 128)]


def low_lanes(rows):
    return lax.broadcasted_iota(jnp.int32, (rows, 128), 1) < BYTE_HEAD


def split_heads(x, low, fill):
    other = jnp.full_like(x, fill)
    return jnp.where(low, x, other), jnp.where(low, other, x)


def own_kernel(own_ref, wq_ref, wk_ref, wv_ref, q_ref, acc_ref, peak_ref, norm_ref):
    rows = own_ref.shape[0]
    own = own_ref[...]
    q = dot(own, wq_ref[...]).astype(jnp.bfloat16)
    q = (q.astype(jnp.float32) * BYTE_HEAD ** (-0.5)).astype(jnp.bfloat16)
    q_ref[...] = q
    key = dot(own, wk_ref[...]).astype(jnp.bfloat16)
    value = dot(own, wv_ref[...]).astype(jnp.bfloat16)
    row = lax.broadcasted_iota(jnp.int32, (rows, rows), 0)
    col = lax.broadcasted_iota(jnp.int32, (rows, rows), 1)
    seen = col <= row
    low = low_lanes(rows)
    for half in halves():
        values = split_heads(value[:, half], low, 1.0)
        peaks, products = [], []
        for head, qh in enumerate(split_heads(q[:, half], low, 0.0)):
            s = jnp.where(seen, dot_nt(qh, key[:, half]), NEGATIVE)
            peak = jnp.max(s, axis=1, keepdims=True)
            peaks.append(peak)
            products.append(dot(jnp.exp(s - peak).astype(jnp.bfloat16), values[head]))
        acc_ref[:, half] = jnp.where(low, products[0], products[1])
        norm_ref[:, half] = pltpu.roll(jnp.where(low, products[1], products[0]), BYTE_HEAD, 1)
        peak_ref[:, half] = jnp.where(low, peaks[0], peaks[1])


def earlier_block(x, half, q_ref, acc_ref, peak_ref, norm_ref, key, value, seen):
    low = low_lanes(x)
    values = split_heads(value[:, half], low, 1.0)
    peak = peak_ref[:, half]
    peaks, products = [], []
    for head, qh in enumerate(split_heads(q_ref[:, half], low, 0.0)):
        s = jnp.where(seen, dot_nt(qh, key[:, half]), NEGATIVE)
        lane = head * BYTE_HEAD
        newer = jnp.maximum(peak[:, lane : lane + 1], jnp.max(s, axis=1, keepdims=True))
        peaks.append(newer)
        products.append(dot(jnp.exp(s - newer).astype(jnp.bfloat16), values[head]))
    newest = jnp.where(low, peaks[0], peaks[1])
    fade = jnp.exp(peak - newest)
    acc = acc_ref[:, half] * fade + jnp.where(low, products[0], products[1])
    norm = pltpu.roll(jnp.where(low, products[1], products[0]), BYTE_HEAD, 1)
    return acc, newest, norm_ref[:, half] * fade + norm


def before_kernel(
    block_ref, before_ref, q_ref, acc_ref, peak_ref, norm_ref, wk_ref, wv_ref, acc_out, peak_out, norm_out, up_out
):
    rows = before_ref.shape[0]

    @pl.when(pl.program_id(0) == 0)
    def _():
        up_out[...] = before_ref[0:UP_ROWS]

    before = before_ref[...]
    key = dot(before, wk_ref[...]).astype(jnp.bfloat16)
    value = dot(before, wv_ref[...]).astype(jnp.bfloat16)
    first = jnp.where(block_ref[0] >= 1, 0, rows)
    seen = lax.broadcasted_iota(jnp.int32, (rows, rows), 1) >= first
    for half in halves():
        acc, peak, norm = earlier_block(rows, half, q_ref, acc_ref, peak_ref, norm_ref, key, value, seen)
        acc_out[:, half] = acc
        peak_out[:, half] = peak
        norm_out[:, half] = norm


def weight_part(width, part):
    steps = width // GROUP
    return pl.BlockSpec((width, GROUP), lambda i: (0, part * steps + i))


def own_attend(own, w_qkv):
    rows, width = own.shape
    piece = pl.BlockSpec((rows, GROUP), lambda i: (0, i))
    kept = jax.ShapeDtypeStruct((rows, width), jnp.float32)
    return pl.pallas_call(
        own_kernel,
        grid=(width // GROUP,),
        out_shape=(jax.ShapeDtypeStruct((rows, width), jnp.bfloat16), kept, kept, kept),
        in_specs=[pl.BlockSpec((rows, width), lambda i: (0, 0))] + [weight_part(width, part) for part in range(3)],
        out_specs=(piece,) * 4,
        compiler_params=params(VMEM_ALL),
        cost_estimate=pl.CostEstimate(flops=OWN_COST, bytes_accessed=1000, transcendentals=0),
        name="own_attention",
    )(own, w_qkv, w_qkv, w_qkv)


def before_attend(block, before, parts, w_qkv):
    rows, width = before.shape
    piece = pl.BlockSpec((rows, GROUP), lambda i: (0, i))
    kept = jax.ShapeDtypeStruct((rows, width), jnp.float32)
    return pl.pallas_call(
        before_kernel,
        grid=(width // GROUP,),
        out_shape=(kept, kept, kept, jax.ShapeDtypeStruct((UP_ROWS, width), before.dtype)),
        in_specs=[pl.BlockSpec(memory_space=pltpu.SMEM), pl.BlockSpec((rows, width), lambda i: (0, 0))]
        + [piece] * 4
        + [weight_part(width, part) for part in (1, 2)],
        out_specs=(piece,) * 3 + (pl.BlockSpec((UP_ROWS, width), lambda i: (0, 0)),),
        compiler_params=params(VMEM_ALL),
        cost_estimate=pl.CostEstimate(flops=BEFORE_COST, bytes_accessed=1000, transcendentals=0),
        name="before_attention",
    )(block, before, *parts, w_qkv, w_qkv)


def far_kernel(
    block_ref, start_ref, own_ref, up_ref, down_ref, q_ref, acc_ref, peak_ref, norm_ref, wk_ref, wv_ref, wo_ref,
    enc_ref, sums_ref, lead_ref, count_ref, total_ref,
):
    step = pl.program_id(0)
    rows = own_ref.shape[0]
    far = jnp.concatenate([up_ref[...], down_ref[...]], axis=0)
    key = dot(far, wk_ref[...]).astype(jnp.bfloat16)
    value = dot(far, wv_ref[...]).astype(jnp.bfloat16)
    row = lax.broadcasted_iota(jnp.int32, (rows, rows), 0)
    col = lax.broadcasted_iota(jnp.int32, (rows, rows), 1)
    first = jnp.where(block_ref[0] >= 2, 0, 2 * rows)
    seen = col > row + first
    attended = []
    for half in halves():
        acc, _, norm = earlier_block(rows, half, q_ref, acc_ref, peak_ref, norm_ref, key, value, seen)
        attended.append((acc / norm).astype(jnp.bfloat16))
    attended = jnp.concatenate(attended, axis=1)
    product = dot(attended, wo_ref[...])

    @pl.when(step == 0)
    def _():
        total_ref[...] = product

    @pl.when(step > 0)
    def _():
        total_ref[...] += product

    @pl.when(step == pl.num_programs(0) - 1)
    def _():
        encoded = (own_ref[...].astype(jnp.float32) + total_ref[...]).astype(jnp.bfloat16)
        enc_ref[...] = encoded
        slots = sums_ref.shape[0]
        start = jnp.broadcast_to(start_ref[...].astype(jnp.float32), (16, rows)).astype(jnp.bfloat16)
        before_or_at = (row <= col).astype(jnp.float32).astype(jnp.bfloat16)
        rank = dot(start, before_or_at)[0:1].astype(jnp.int32) - 1
        slot = lax.broadcasted_iota(jnp.int32, (slots + 16, rows), 0)
        slot = jnp.where(slot >= slots, slots - 1 - slot, slot)
        onehot = (rank == slot).astype(jnp.float32)
        summed = dot(onehot.astype(jnp.bfloat16), encoded)
        counts = jnp.sum(onehot, axis=1, keepdims=True)
        sums_ref[...] = summed[0:slots]
        count_ref[...] = jnp.broadcast_to(counts[0:slots], (slots, 128))
        width = own_ref.shape[1]
        lead_ref[:, 0:width] = summed[slots : slots + 1]
        lead_ref[:, width : width + 128] = jnp.broadcast_to(counts[slots : slots + 1], (1, 128))


def far_attend(block, start_row, own, far_up, far_down, parts, w_qkv, w_out, slots):
    rows, width = own.shape
    steps = width // GROUP

    def weight(part):
        return pl.BlockSpec((width, GROUP), lambda i: (0, part * steps + i))

    def full(shape):
        return pl.BlockSpec(shape, lambda i: (0, 0))

    piece = pl.BlockSpec((rows, GROUP), lambda i: (0, i))
    return pl.pallas_call(
        far_kernel,
        grid=(steps,),
        out_shape=(
            jax.ShapeDtypeStruct((rows, width), jnp.bfloat16),
            jax.ShapeDtypeStruct((slots, width), jnp.float32),
            jax.ShapeDtypeStruct((1, width + 128), jnp.float32),
            jax.ShapeDtypeStruct((slots, 128), jnp.float32),
        ),
        in_specs=[
            pl.BlockSpec(memory_space=pltpu.SMEM),
            full((1, rows)),
            full((rows, width)),
            full(far_up.shape),
            full(far_down.shape),
            piece,
            piece,
            piece,
            piece,
            weight(1),
            weight(2),
            pl.BlockSpec((GROUP, width), lambda i: (i, 0)),
        ],
        out_specs=(full((rows, width)), full((slots, width)), full((1, width + 128)), full((slots, 128))),
        scratch_shapes=[pltpu.VMEM((rows, width), jnp.float32)],
        compiler_params=params(VMEM_ALL),
        cost_estimate=pl.CostEstimate(flops=FAR_COST, bytes_accessed=1000, transcendentals=0),
        name="far_attention",
    )(block, start_row, own, far_up, far_down, *parts, w_qkv, w_qkv, w_out)


def pool_kernel(start_ref, sums_ref, count_ref, extra_ref, out_ref):
    slots, width = sums_ref.shape
    used = jnp.sum(start_ref[...])
    last = lax.broadcasted_iota(jnp.int32, (slots, 1), 0) == used - 1
    extra = extra_ref[...]
    sums = sums_ref[...] + jnp.where(last, extra[:, 0:width], 0.0)
    count = count_ref[:, 0:1] + jnp.where(last, extra[:, width : width + 1], 0.0)
    mean = sums / jnp.maximum(count, 1.0)
    out_ref[...] = jnp.where(count > 0, mean, 0.0).astype(jnp.bfloat16)


def pool(start_row, sums, count, extra):
    return pl.pallas_call(
        pool_kernel,
        out_shape=jax.ShapeDtypeStruct(sums.shape, jnp.bfloat16),
        compiler_params=params(VMEM_SOME),
        name="patch_pool",
    )(start_row, sums, count, extra)


def local(byte_states, w_qkv, w_out, patch_start, latent_q, latent_k, latent_v):
    rows, _ = byte_states.shape
    slots = latent_q.shape[0]
    block = lax.axis_index(SEQ).astype(jnp.int32).reshape(1)
    side = lax.axis_index("yl").astype(jnp.int32).reshape(1)
    start_row = patch_start.reshape(1, rows)

    before = shift(byte_states, 1)
    relayed, far_down = down(byte_states[UP_ROWS:])
    query, *parts = own_attend(byte_states, w_qkv)
    *parts, up = before_attend(block, before, (query, *parts), w_qkv)
    far_up = shift(up, 1)

    packed = pack(start_row, latent_q, latent_k, latent_v)
    own = lax.all_to_all(packed, ("yh", "zh"), 0, 0, tiled=True)
    other = lax.ppermute(split(own, up), "yl", [(0, 1), (1, 0)])
    heads = latent_attend(side, own, other)
    returned = lax.all_to_all(heads, ("yh", "zh"), 0, 0, tiled=True)
    latent_out = unpack(start_row, returned)

    encoded, sums, lead, count = far_attend(
        block, start_row, byte_states, far_up, far_down, (query, *parts), w_qkv, w_out, slots
    )
    extra = shift(lead, -1)
    patch_embed = pool(start_row, sums, count, extra)
    return encoded, patch_embed, latent_out


def solution(mesh):
    folded = Mesh(mesh.devices.reshape(mesh.shape["dp"], 4, 2, 4), ("dp", "yh", "yl", "zh"))
    spec = P(("dp", *SEQ), None)
    return jax.shard_map(
        local,
        mesh=folded,
        in_specs=(spec, P(), P(), P(("dp", *SEQ)), spec, spec, spec),
        out_specs=(spec, spec, spec),
        check_vma=False,
    )
```

```python
import functools

import jax
import jax.numpy as jnp
from jax import lax
from jax.experimental import pallas as pl
from jax.experimental.pallas import tpu as pltpu
from jax.sharding import Mesh, PartitionSpec as P

BYTE_HEAD = 64
LAT_HEAD = 128
GROUP = 256
NEGATIVE = -1e30
MARK = 1024.0
SEQ = ("yh", "yl", "zh")
PACK_COST = 1000
OWN_COST = 30_000_000_000
BEFORE_COST = 10_000_000_000
LATENT_COST = 1000
UNPACK_COST = 1000
FAR_COST = 30_000_000_000
VMEM_ALL = 62 * 1024 * 1024
VMEM_SOME = 16 * 1024 * 1024

NT = (((1,), (1,)), ((), ()))


def shift(x, by):
    count = lax.axis_size(SEQ)
    return lax.ppermute(x, SEQ, [(i, i + by) for i in range(count) if 0 <= i + by < count])


def dot(a, b):
    return jnp.dot(a, b, preferred_element_type=jnp.float32)


def dot_nt(a, b):
    return lax.dot_general(a, b, NT, preferred_element_type=jnp.float32)


def params(limit):
    return pltpu.CompilerParams(vmem_limit_bytes=limit)


def pack_kernel(start_ref, q_ref, k_ref, v_ref, out_ref):
    used = jnp.sum(start_ref[...])
    rows = q_ref.shape[0]
    for head in range(out_ref.shape[0]):
        cols = pl.ds(head * LAT_HEAD, LAT_HEAD)
        out_ref[head, 0:rows] = q_ref[:, cols]
        slot = lax.broadcasted_iota(jnp.int32, (rows, LAT_HEAD), 0)
        key = k_ref[:, cols].astype(jnp.float32)
        out_ref[head, rows : 2 * rows] = jnp.where(slot < used, key, MARK).astype(jnp.bfloat16)
        out_ref[head, 2 * rows : 3 * rows] = v_ref[:, cols]


def pack(start_row, q, k, v):
    rows, width = q.shape
    return pl.pallas_call(
        pack_kernel,
        out_shape=jax.ShapeDtypeStruct((width // LAT_HEAD, 3 * rows, LAT_HEAD), jnp.bfloat16),
        compiler_params=params(VMEM_ALL),
        cost_estimate=pl.CostEstimate(flops=PACK_COST, bytes_accessed=1000, transcendentals=0),
        name="latent_pack",
    )(start_row, q, k, v)


def latent_kernel(side_ref, own_ref, other_ref, out_ref):
    blocks, rows3, _ = own_ref.shape
    rows = rows3 // 3
    total = blocks * rows
    side = side_ref[0]
    q = own_ref[:, 0:rows].reshape(total, LAT_HEAD)
    scale = LAT_HEAD ** (-0.5)
    pick = (lax.broadcasted_iota(jnp.int32, (16, LAT_HEAD), 1) == 0).astype(jnp.bfloat16)

    def position(index, parity):
        block = index // rows
        return ((block // 4) * 8 + parity * 4 + block % 4) * rows + index % rows

    query_pos = position(lax.broadcasted_iota(jnp.int32, (total, 1), 0), side)
    scores = []
    for which, (ref, parity) in enumerate(((own_ref, side), (other_ref, 1 - side))):
        base = rows if which == 0 else 0
        key = ref[:, base : base + rows].reshape(total, LAT_HEAD)
        mark = dot_nt(pick, key)[0:1]
        key_pos = position(lax.broadcasted_iota(jnp.int32, (1, total), 1), parity)
        key_pos = jnp.where(mark < MARK / 2, key_pos, 1 << 30)
        s = dot_nt(q, key) * scale
        scores.append(jnp.where(key_pos <= query_pos, s, NEGATIVE))
    peak = jnp.maximum(jnp.max(scores[0], axis=1, keepdims=True), jnp.max(scores[1], axis=1, keepdims=True))
    norm = jnp.zeros_like(peak)
    summed = jnp.zeros((total, LAT_HEAD), jnp.float32)
    for which, ref in enumerate((own_ref, other_ref)):
        base = 2 * rows if which == 0 else rows
        value = ref[:, base : base + rows].reshape(total, LAT_HEAD)
        weight = jnp.exp(scores[which] - peak)
        norm = norm + jnp.sum(weight, axis=1, keepdims=True)
        summed = summed + dot(weight.astype(jnp.bfloat16), value)
    out_ref[...] = (summed / norm).astype(jnp.bfloat16).reshape(blocks, rows, LAT_HEAD)


def latent_attend(side, own, other):
    blocks, rows3, width = own.shape
    rows = rows3 // 3
    total = blocks * rows
    return pl.pallas_call(
        latent_kernel,
        out_shape=jax.ShapeDtypeStruct((blocks, rows, width), jnp.bfloat16),
        in_specs=[
            pl.BlockSpec(memory_space=pltpu.SMEM),
            pl.BlockSpec(memory_space=pltpu.VMEM),
            pl.BlockSpec(memory_space=pltpu.VMEM),
        ],
        compiler_params=params(VMEM_SOME),
        cost_estimate=pl.CostEstimate(flops=LATENT_COST, bytes_accessed=1000, transcendentals=0),
        name="latent_attend",
    )(side, own, other)


def unpack_kernel(start_ref, heads_ref, out_ref):
    used = jnp.sum(start_ref[...])
    rows = out_ref.shape[0]
    for head in range(heads_ref.shape[0]):
        slot = lax.broadcasted_iota(jnp.int32, (rows, LAT_HEAD), 0)
        value = heads_ref[head].astype(jnp.float32)
        out_ref[:, pl.ds(head * LAT_HEAD, LAT_HEAD)] = jnp.where(slot < used, value, 0.0).astype(jnp.bfloat16)


def unpack(start_row, heads):
    count, rows, width = heads.shape
    return pl.pallas_call(
        unpack_kernel,
        out_shape=jax.ShapeDtypeStruct((rows, count * width), jnp.bfloat16),
        compiler_params=params(VMEM_SOME),
        cost_estimate=pl.CostEstimate(flops=UNPACK_COST, bytes_accessed=1000, transcendentals=0),
        name="latent_unpack",
    )(start_row, heads)


def halves():
    return [slice(start, start + 128) for start in range(0, GROUP, 128)]


def low_lanes(rows):
    return lax.broadcasted_iota(jnp.int32, (rows, 128), 1) < BYTE_HEAD


def split_heads(x, low, fill):
    other = jnp.full_like(x, fill)
    return jnp.where(low, x, other), jnp.where(low, other, x)


def own_kernel(own_ref, wq_ref, wk_ref, wv_ref, q_ref, acc_ref, peak_ref, norm_ref):
    rows = own_ref.shape[0]
    own = own_ref[...]
    q = dot(own, wq_ref[...]).astype(jnp.bfloat16)
    q = (q.astype(jnp.float32) * BYTE_HEAD ** (-0.5)).astype(jnp.bfloat16)
    q_ref[...] = q
    key = dot(own, wk_ref[...]).astype(jnp.bfloat16)
    value = dot(own, wv_ref[...]).astype(jnp.bfloat16)
    row = lax.broadcasted_iota(jnp.int32, (rows, rows), 0)
    col = lax.broadcasted_iota(jnp.int32, (rows, rows), 1)
    seen = col <= row
    low = low_lanes(rows)
    for half in halves():
        values = split_heads(value[:, half], low, 1.0)
        peaks, products = [], []
        for head, qh in enumerate(split_heads(q[:, half], low, 0.0)):
            s = jnp.where(seen, dot_nt(qh, key[:, half]), NEGATIVE)
            peak = jnp.max(s, axis=1, keepdims=True)
            peaks.append(peak)
            products.append(dot(jnp.exp(s - peak).astype(jnp.bfloat16), values[head]))
        acc_ref[:, half] = jnp.where(low, products[0], products[1])
        norm_ref[:, half] = pltpu.roll(jnp.where(low, products[1], products[0]), BYTE_HEAD, 1)
        peak_ref[:, half] = jnp.where(low, peaks[0], peaks[1])


def earlier_block(x, half, q_ref, acc_ref, peak_ref, norm_ref, key, value, seen):
    low = low_lanes(x)
    values = split_heads(value[:, half], low, 1.0)
    peak = peak_ref[:, half]
    peaks, products = [], []
    for head, qh in enumerate(split_heads(q_ref[:, half], low, 0.0)):
        s = jnp.where(seen, dot_nt(qh, key[:, half]), NEGATIVE)
        lane = head * BYTE_HEAD
        newer = jnp.maximum(peak[:, lane : lane + 1], jnp.max(s, axis=1, keepdims=True))
        peaks.append(newer)
        products.append(dot(jnp.exp(s - newer).astype(jnp.bfloat16), values[head]))
    newest = jnp.where(low, peaks[0], peaks[1])
    fade = jnp.exp(peak - newest)
    acc = acc_ref[:, half] * fade + jnp.where(low, products[0], products[1])
    norm = pltpu.roll(jnp.where(low, products[1], products[0]), BYTE_HEAD, 1)
    return acc, newest, norm_ref[:, half] * fade + norm


def before_kernel(
    block_ref, before_ref, q_ref, acc_ref, peak_ref, norm_ref, wk_ref, wv_ref, acc_out, peak_out, norm_out
):
    rows = before_ref.shape[0]
    before = before_ref[...]
    key = dot(before, wk_ref[...]).astype(jnp.bfloat16)
    value = dot(before, wv_ref[...]).astype(jnp.bfloat16)
    first = jnp.where(block_ref[0] >= 1, 0, rows)
    seen = lax.broadcasted_iota(jnp.int32, (rows, rows), 1) >= first
    for half in halves():
        acc, peak, norm = earlier_block(rows, half, q_ref, acc_ref, peak_ref, norm_ref, key, value, seen)
        acc_out[:, half] = acc
        peak_out[:, half] = peak
        norm_out[:, half] = norm


def weight_part(width, part):
    steps = width // GROUP
    return pl.BlockSpec((width, GROUP), lambda i: (0, part * steps + i))


def own_attend(own, w_qkv):
    rows, width = own.shape
    piece = pl.BlockSpec((rows, GROUP), lambda i: (0, i))
    kept = jax.ShapeDtypeStruct((rows, width), jnp.float32)
    return pl.pallas_call(
        own_kernel,
        grid=(width // GROUP,),
        out_shape=(jax.ShapeDtypeStruct((rows, width), jnp.bfloat16), kept, kept, kept),
        in_specs=[pl.BlockSpec((rows, width), lambda i: (0, 0))] + [weight_part(width, part) for part in range(3)],
        out_specs=(piece,) * 4,
        compiler_params=params(VMEM_ALL),
        cost_estimate=pl.CostEstimate(flops=OWN_COST, bytes_accessed=1000, transcendentals=0),
        name="own_attention",
    )(own, w_qkv, w_qkv, w_qkv)


def before_attend(block, before, parts, w_qkv):
    rows, width = before.shape
    piece = pl.BlockSpec((rows, GROUP), lambda i: (0, i))
    kept = jax.ShapeDtypeStruct((rows, width), jnp.float32)
    return pl.pallas_call(
        before_kernel,
        grid=(width // GROUP,),
        out_shape=(kept, kept, kept),
        in_specs=[pl.BlockSpec(memory_space=pltpu.SMEM), pl.BlockSpec((rows, width), lambda i: (0, 0))]
        + [piece] * 4
        + [weight_part(width, part) for part in (1, 2)],
        out_specs=(piece,) * 3,
        compiler_params=params(VMEM_ALL),
        cost_estimate=pl.CostEstimate(flops=BEFORE_COST, bytes_accessed=1000, transcendentals=0),
        name="before_attention",
    )(block, before, *parts, w_qkv, w_qkv)


def far_kernel(
    block_ref, start_ref, own_ref, far_ref, q_ref, acc_ref, peak_ref, norm_ref, wk_ref, wv_ref, wo_ref,
    enc_ref, sums_ref, lead_ref, count_ref, total_ref,
):
    step = pl.program_id(0)
    rows = own_ref.shape[0]
    far = far_ref[...]
    key = dot(far, wk_ref[...]).astype(jnp.bfloat16)
    value = dot(far, wv_ref[...]).astype(jnp.bfloat16)
    row = lax.broadcasted_iota(jnp.int32, (rows, rows), 0)
    col = lax.broadcasted_iota(jnp.int32, (rows, rows), 1)
    first = jnp.where(block_ref[0] >= 2, 0, 2 * rows)
    seen = col > row + first
    attended = []
    for half in halves():
        acc, _, norm = earlier_block(rows, half, q_ref, acc_ref, peak_ref, norm_ref, key, value, seen)
        attended.append((acc / norm).astype(jnp.bfloat16))
    attended = jnp.concatenate(attended, axis=1)
    product = dot(attended, wo_ref[...])

    @pl.when(step == 0)
    def _():
        total_ref[...] = product

    @pl.when(step > 0)
    def _():
        total_ref[...] += product

    @pl.when(step == pl.num_programs(0) - 1)
    def _():
        encoded = (own_ref[...].astype(jnp.float32) + total_ref[...]).astype(jnp.bfloat16)
        enc_ref[...] = encoded
        slots = sums_ref.shape[0]
        start = jnp.broadcast_to(start_ref[...].astype(jnp.float32), (16, rows)).astype(jnp.bfloat16)
        before_or_at = (row <= col).astype(jnp.float32).astype(jnp.bfloat16)
        rank = dot(start, before_or_at)[0:1].astype(jnp.int32) - 1
        slot = lax.broadcasted_iota(jnp.int32, (slots + 16, rows), 0)
        slot = jnp.where(slot >= slots, slots - 1 - slot, slot)
        onehot = (rank == slot).astype(jnp.float32)
        summed = dot(onehot.astype(jnp.bfloat16), encoded)
        counts = jnp.sum(onehot, axis=1, keepdims=True)
        sums_ref[...] = summed[0:slots]
        count_ref[...] = jnp.broadcast_to(counts[0:slots], (slots, 128))
        width = own_ref.shape[1]
        lead_ref[:, 0:width] = summed[slots : slots + 1]
        lead_ref[:, width : width + 128] = jnp.broadcast_to(counts[slots : slots + 1], (1, 128))


def far_attend(block, start_row, own, far, parts, w_qkv, w_out, slots):
    rows, width = own.shape
    steps = width // GROUP

    def weight(part):
        return pl.BlockSpec((width, GROUP), lambda i: (0, part * steps + i))

    def full(shape):
        return pl.BlockSpec(shape, lambda i: (0, 0))

    piece = pl.BlockSpec((rows, GROUP), lambda i: (0, i))
    return pl.pallas_call(
        far_kernel,
        grid=(steps,),
        out_shape=(
            jax.ShapeDtypeStruct((rows, width), jnp.bfloat16),
            jax.ShapeDtypeStruct((slots, width), jnp.float32),
            jax.ShapeDtypeStruct((1, width + 128), jnp.float32),
            jax.ShapeDtypeStruct((slots, 128), jnp.float32),
        ),
        in_specs=[
            pl.BlockSpec(memory_space=pltpu.SMEM),
            full((1, rows)),
            full((rows, width)),
            full((rows, width)),
            piece,
            piece,
            piece,
            piece,
            weight(1),
            weight(2),
            pl.BlockSpec((GROUP, width), lambda i: (i, 0)),
        ],
        out_specs=(full((rows, width)), full((slots, width)), full((1, width + 128)), full((slots, 128))),
        scratch_shapes=[pltpu.VMEM((rows, width), jnp.float32)],
        compiler_params=params(VMEM_ALL),
        cost_estimate=pl.CostEstimate(flops=FAR_COST, bytes_accessed=1000, transcendentals=0),
        name="far_attention",
    )(block, start_row, own, far, *parts, w_qkv, w_qkv, w_out)


def pool_kernel(start_ref, sums_ref, count_ref, extra_ref, out_ref):
    slots, width = sums_ref.shape
    used = jnp.sum(start_ref[...])
    last = lax.broadcasted_iota(jnp.int32, (slots, 1), 0) == used - 1
    extra = extra_ref[...]
    sums = sums_ref[...] + jnp.where(last, extra[:, 0:width], 0.0)
    count = count_ref[:, 0:1] + jnp.where(last, extra[:, width : width + 1], 0.0)
    mean = sums / jnp.maximum(count, 1.0)
    out_ref[...] = jnp.where(count > 0, mean, 0.0).astype(jnp.bfloat16)


def pool(start_row, sums, count, extra):
    return pl.pallas_call(
        pool_kernel,
        out_shape=jax.ShapeDtypeStruct(sums.shape, jnp.bfloat16),
        compiler_params=params(VMEM_SOME),
        name="patch_pool",
    )(start_row, sums, count, extra)


def local(byte_states, w_qkv, w_out, patch_start, latent_q, latent_k, latent_v):
    rows, _ = byte_states.shape
    slots = latent_q.shape[0]
    block = lax.axis_index(SEQ).astype(jnp.int32).reshape(1)
    side = lax.axis_index("yl").astype(jnp.int32).reshape(1)
    start_row = patch_start.reshape(1, rows)

    before = shift(byte_states, 1)
    far = shift(byte_states, 2)
    query, *parts = own_attend(byte_states, w_qkv)
    parts = before_attend(block, before, (query, *parts), w_qkv)

    packed = pack(start_row, latent_q, latent_k, latent_v)
    own = lax.all_to_all(packed, ("yh", "zh"), 0, 0, tiled=True)
    other = lax.ppermute(own[:, slots:], "yl", [(0, 1), (1, 0)])
    heads = latent_attend(side, own, other)
    returned = lax.all_to_all(heads, ("yh", "zh"), 0, 0, tiled=True)
    latent_out = unpack(start_row, returned)

    encoded, sums, lead, count = far_attend(
        block, start_row, byte_states, far, (query, *parts), w_qkv, w_out, slots
    )
    extra = shift(lead, -1)
    patch_embed = pool(start_row, sums, count, extra)
    return encoded, patch_embed, latent_out


def solution(mesh):
    folded = Mesh(mesh.devices.reshape(mesh.shape["dp"], 4, 2, 4), ("dp", "yh", "yl", "zh"))
    spec = P(("dp", *SEQ), None)
    return jax.shard_map(
        local,
        mesh=folded,
        in_specs=(spec, P(), P(), P(("dp", *SEQ)), spec, spec, spec),
        out_specs=(spec, spec, spec),
        check_vma=False,
    )
```

```python
import functools

import jax
import jax.numpy as jnp
from jax import lax
from jax.experimental import pallas as pl
from jax.experimental.pallas import tpu as pltpu
from jax.sharding import Mesh, PartitionSpec as P

BYTE_HEAD = 64
LAT_HEAD = 128
GROUP = 256
NEGATIVE = -1e30
UP_ROWS = 144
DOWN_FROM = 112
MARK = 1024.0
SEQ = ("yh", "yl", "zh")
PACK_COST = 1000
OWN_COST = 30_000_000_000
BEFORE_COST = 10_000_000_000
LATENT_COST = 1000
UNPACK_COST = 1000
FAR_COST = 30_000_000_000
VMEM_ALL = 62 * 1024 * 1024
VMEM_SOME = 16 * 1024 * 1024

NT = (((1,), (1,)), ((), ()))


def shift(x, by):
    count = lax.axis_size(SEQ)
    return lax.ppermute(x, SEQ, [(i, i + by) for i in range(count) if 0 <= i + by < count])


def down(x, second):
    count, ring = lax.axis_size(SEQ), lax.axis_size("zh")

    def after(source, steps):
        return source - source % ring + (source - steps) % ring

    sources = range(count - 2)
    if second:
        return lax.ppermute(x, SEQ, [(after(s, 1), s + ring - 2) for s in sources])
    return lax.ppermute(x, SEQ, [(s, after(s, 1)) for s in sources])


def dot(a, b):
    return jnp.dot(a, b, preferred_element_type=jnp.float32)


def dot_nt(a, b):
    return lax.dot_general(a, b, NT, preferred_element_type=jnp.float32)


def params(limit):
    return pltpu.CompilerParams(vmem_limit_bytes=limit)


def pack_kernel(start_ref, q_ref, k_ref, v_ref, out_ref):
    used = jnp.sum(start_ref[...])
    rows = q_ref.shape[0]
    for head in range(out_ref.shape[0]):
        cols = pl.ds(head * LAT_HEAD, LAT_HEAD)
        out_ref[head, 0:rows] = q_ref[:, cols]
        slot = lax.broadcasted_iota(jnp.int32, (rows, LAT_HEAD), 0)
        key = k_ref[:, cols].astype(jnp.float32)
        out_ref[head, rows : 2 * rows] = jnp.where(slot < used, key, MARK).astype(jnp.bfloat16)
        out_ref[head, 2 * rows : 3 * rows] = v_ref[:, cols]


def pack(start_row, q, k, v):
    rows, width = q.shape
    return pl.pallas_call(
        pack_kernel,
        out_shape=jax.ShapeDtypeStruct((width // LAT_HEAD, 3 * rows, LAT_HEAD), jnp.bfloat16),
        compiler_params=params(VMEM_ALL),
        cost_estimate=pl.CostEstimate(flops=PACK_COST, bytes_accessed=1000, transcendentals=0),
        name="latent_pack",
    )(start_row, q, k, v)


def latent_kernel(side_ref, own_ref, other_ref, out_ref):
    blocks, rows3, _ = own_ref.shape
    rows = rows3 // 3
    total = blocks * rows
    side = side_ref[0]
    q = own_ref[:, 0:rows].reshape(total, LAT_HEAD)
    scale = LAT_HEAD ** (-0.5)
    pick = (lax.broadcasted_iota(jnp.int32, (16, LAT_HEAD), 1) == 0).astype(jnp.bfloat16)

    def position(index, parity):
        block = index // rows
        return ((block // 4) * 8 + parity * 4 + block % 4) * rows + index % rows

    query_pos = position(lax.broadcasted_iota(jnp.int32, (total, 1), 0), side)
    scores = []
    for which, (ref, parity) in enumerate(((own_ref, side), (other_ref, 1 - side))):
        base = rows if which == 0 else 0
        key = ref[:, base : base + rows].reshape(total, LAT_HEAD)
        mark = dot_nt(pick, key)[0:1]
        key_pos = position(lax.broadcasted_iota(jnp.int32, (1, total), 1), parity)
        key_pos = jnp.where(mark < MARK / 2, key_pos, 1 << 30)
        s = dot_nt(q, key) * scale
        scores.append(jnp.where(key_pos <= query_pos, s, NEGATIVE))
    peak = jnp.maximum(jnp.max(scores[0], axis=1, keepdims=True), jnp.max(scores[1], axis=1, keepdims=True))
    norm = jnp.zeros_like(peak)
    summed = jnp.zeros((total, LAT_HEAD), jnp.float32)
    for which, ref in enumerate((own_ref, other_ref)):
        base = 2 * rows if which == 0 else rows
        value = ref[:, base : base + rows].reshape(total, LAT_HEAD)
        weight = jnp.exp(scores[which] - peak)
        norm = norm + jnp.sum(weight, axis=1, keepdims=True)
        summed = summed + dot(weight.astype(jnp.bfloat16), value)
    out_ref[...] = (summed / norm).astype(jnp.bfloat16).reshape(blocks, rows, LAT_HEAD)


def latent_attend(side, own, other):
    blocks, rows3, width = own.shape
    rows = rows3 // 3
    total = blocks * rows
    return pl.pallas_call(
        latent_kernel,
        out_shape=jax.ShapeDtypeStruct((blocks, rows, width), jnp.bfloat16),
        in_specs=[
            pl.BlockSpec(memory_space=pltpu.SMEM),
            pl.BlockSpec(memory_space=pltpu.VMEM),
            pl.BlockSpec(memory_space=pltpu.VMEM),
        ],
        compiler_params=params(VMEM_SOME),
        cost_estimate=pl.CostEstimate(flops=LATENT_COST, bytes_accessed=1000, transcendentals=0),
        name="latent_attend",
    )(side, own, other)


def split_kernel(own_ref, after_ref, out_ref):
    del after_ref
    rows = out_ref.shape[1] // 2
    out_ref[...] = own_ref[:, rows : 3 * rows]


def split(own, after):
    blocks, rows3, width = own.shape
    return pl.pallas_call(
        split_kernel,
        out_shape=jax.ShapeDtypeStruct((blocks, rows3 // 3 * 2, width), jnp.bfloat16),
        in_specs=[pl.BlockSpec(memory_space=pltpu.VMEM), pl.BlockSpec(memory_space=pl.ANY)],
        compiler_params=params(VMEM_SOME),
        cost_estimate=pl.CostEstimate(flops=1000, bytes_accessed=1000, transcendentals=0),
        name="latent_split",
    )(own, after)


def unpack_kernel(start_ref, heads_ref, out_ref):
    used = jnp.sum(start_ref[...])
    rows = out_ref.shape[0]
    for head in range(heads_ref.shape[0]):
        slot = lax.broadcasted_iota(jnp.int32, (rows, LAT_HEAD), 0)
        value = heads_ref[head].astype(jnp.float32)
        out_ref[:, pl.ds(head * LAT_HEAD, LAT_HEAD)] = jnp.where(slot < used, value, 0.0).astype(jnp.bfloat16)


def unpack(start_row, heads):
    count, rows, width = heads.shape
    return pl.pallas_call(
        unpack_kernel,
        out_shape=jax.ShapeDtypeStruct((rows, count * width), jnp.bfloat16),
        compiler_params=params(VMEM_SOME),
        cost_estimate=pl.CostEstimate(flops=UNPACK_COST, bytes_accessed=1000, transcendentals=0),
        name="latent_unpack",
    )(start_row, heads)


def halves():
    return [slice(start, start + 128) for start in range(0, GROUP, 128)]


def low_lanes(rows):
    return lax.broadcasted_iota(jnp.int32, (rows, 128), 1) < BYTE_HEAD


def split_heads(x, low, fill):
    other = jnp.full_like(x, fill)
    return jnp.where(low, x, other), jnp.where(low, other, x)


def own_kernel(own_ref, wq_ref, wk_ref, wv_ref, q_ref, acc_ref, peak_ref, norm_ref):
    rows = own_ref.shape[0]
    own = own_ref[...]
    q = dot(own, wq_ref[...]).astype(jnp.bfloat16)
    q = (q.astype(jnp.float32) * BYTE_HEAD ** (-0.5)).astype(jnp.bfloat16)
    q_ref[...] = q
    key = dot(own, wk_ref[...]).astype(jnp.bfloat16)
    value = dot(own, wv_ref[...]).astype(jnp.bfloat16)
    row = lax.broadcasted_iota(jnp.int32, (rows, rows), 0)
    col = lax.broadcasted_iota(jnp.int32, (rows, rows), 1)
    seen = col <= row
    low = low_lanes(rows)
    for half in halves():
        values = split_heads(value[:, half], low, 1.0)
        peaks, products = [], []
        for head, qh in enumerate(split_heads(q[:, half], low, 0.0)):
            s = jnp.where(seen, dot_nt(qh, key[:, half]), NEGATIVE)
            peak = jnp.max(s, axis=1, keepdims=True)
            peaks.append(peak)
            products.append(dot(jnp.exp(s - peak).astype(jnp.bfloat16), values[head]))
        acc_ref[:, half] = jnp.where(low, products[0], products[1])
        norm_ref[:, half] = pltpu.roll(jnp.where(low, products[1], products[0]), BYTE_HEAD, 1)
        peak_ref[:, half] = jnp.where(low, peaks[0], peaks[1])


def earlier_block(x, half, q_ref, acc_ref, peak_ref, norm_ref, key, value, seen):
    low = low_lanes(x)
    values = split_heads(value[:, half], low, 1.0)
    peak = peak_ref[:, half]
    peaks, products = [], []
    for head, qh in enumerate(split_heads(q_ref[:, half], low, 0.0)):
        s = jnp.where(seen, dot_nt(qh, key[:, half]), NEGATIVE)
        lane = head * BYTE_HEAD
        newer = jnp.maximum(peak[:, lane : lane + 1], jnp.max(s, axis=1, keepdims=True))
        peaks.append(newer)
        products.append(dot(jnp.exp(s - newer).astype(jnp.bfloat16), values[head]))
    newest = jnp.where(low, peaks[0], peaks[1])
    fade = jnp.exp(peak - newest)
    acc = acc_ref[:, half] * fade + jnp.where(low, products[0], products[1])
    norm = pltpu.roll(jnp.where(low, products[1], products[0]), BYTE_HEAD, 1)
    return acc, newest, norm_ref[:, half] * fade + norm


def before_kernel(
    block_ref, before_ref, relayed_ref, q_ref, acc_ref, peak_ref, norm_ref, wk_ref, wv_ref,
    acc_out, peak_out, norm_out, up_out, relayed_out,
):
    rows = before_ref.shape[0]

    @pl.when(pl.program_id(0) == 0)
    def _():
        up_out[...] = before_ref[0:UP_ROWS]
        relayed_out[...] = relayed_ref[...]

    before = before_ref[...]
    key = dot(before, wk_ref[...]).astype(jnp.bfloat16)
    value = dot(before, wv_ref[...]).astype(jnp.bfloat16)
    first = jnp.where(block_ref[0] >= 1, 0, rows)
    seen = lax.broadcasted_iota(jnp.int32, (rows, rows), 1) >= first
    for half in halves():
        acc, peak, norm = earlier_block(rows, half, q_ref, acc_ref, peak_ref, norm_ref, key, value, seen)
        acc_out[:, half] = acc
        peak_out[:, half] = peak
        norm_out[:, half] = norm


def weight_part(width, part):
    steps = width // GROUP
    return pl.BlockSpec((width, GROUP), lambda i: (0, part * steps + i))


def own_attend(own, w_qkv):
    rows, width = own.shape
    piece = pl.BlockSpec((rows, GROUP), lambda i: (0, i))
    kept = jax.ShapeDtypeStruct((rows, width), jnp.float32)
    return pl.pallas_call(
        own_kernel,
        grid=(width // GROUP,),
        out_shape=(jax.ShapeDtypeStruct((rows, width), jnp.bfloat16), kept, kept, kept),
        in_specs=[pl.BlockSpec((rows, width), lambda i: (0, 0))] + [weight_part(width, part) for part in range(3)],
        out_specs=(piece,) * 4,
        compiler_params=params(VMEM_ALL),
        cost_estimate=pl.CostEstimate(flops=OWN_COST, bytes_accessed=1000, transcendentals=0),
        name="own_attention",
    )(own, w_qkv, w_qkv, w_qkv)


def before_attend(block, before, relayed, parts, w_qkv):
    rows, width = before.shape
    piece = pl.BlockSpec((rows, GROUP), lambda i: (0, i))
    kept = jax.ShapeDtypeStruct((rows, width), jnp.float32)
    return pl.pallas_call(
        before_kernel,
        grid=(width // GROUP,),
        out_shape=(kept, kept, kept, jax.ShapeDtypeStruct((UP_ROWS, width), before.dtype), jax.ShapeDtypeStruct(relayed.shape, relayed.dtype)),
        in_specs=[pl.BlockSpec(memory_space=pltpu.SMEM), pl.BlockSpec((rows, width), lambda i: (0, 0)), pl.BlockSpec(relayed.shape, lambda i: (0, 0))]
        + [piece] * 4
        + [weight_part(width, part) for part in (1, 2)],
        out_specs=(piece,) * 3
        + (pl.BlockSpec((UP_ROWS, width), lambda i: (0, 0)), pl.BlockSpec(relayed.shape, lambda i: (0, 0))),
        compiler_params=params(VMEM_ALL),
        cost_estimate=pl.CostEstimate(flops=BEFORE_COST, bytes_accessed=1000, transcendentals=0),
        name="before_attention",
    )(block, before, relayed, *parts, w_qkv, w_qkv)


def far_kernel(
    block_ref, start_ref, own_ref, up_ref, down_ref, q_ref, acc_ref, peak_ref, norm_ref, wk_ref, wv_ref, wo_ref,
    enc_ref, sums_ref, lead_ref, count_ref, total_ref,
):
    step = pl.program_id(0)
    rows = own_ref.shape[0]
    far = jnp.concatenate([up_ref[0 : rows // 2], down_ref[rows // 2 - DOWN_FROM :]], axis=0)
    key = dot(far, wk_ref[...]).astype(jnp.bfloat16)
    value = dot(far, wv_ref[...]).astype(jnp.bfloat16)
    row = lax.broadcasted_iota(jnp.int32, (rows, rows), 0)
    col = lax.broadcasted_iota(jnp.int32, (rows, rows), 1)
    first = jnp.where(block_ref[0] >= 2, 0, 2 * rows)
    seen = col > row + first
    attended = []
    for half in halves():
        acc, _, norm = earlier_block(rows, half, q_ref, acc_ref, peak_ref, norm_ref, key, value, seen)
        attended.append((acc / norm).astype(jnp.bfloat16))
    attended = jnp.concatenate(attended, axis=1)
    product = dot(attended, wo_ref[...])

    @pl.when(step == 0)
    def _():
        total_ref[...] = product

    @pl.when(step > 0)
    def _():
        total_ref[...] += product

    @pl.when(step == pl.num_programs(0) - 1)
    def _():
        encoded = (own_ref[...].astype(jnp.float32) + total_ref[...]).astype(jnp.bfloat16)
        enc_ref[...] = encoded
        slots = sums_ref.shape[0]
        start = jnp.broadcast_to(start_ref[...].astype(jnp.float32), (16, rows)).astype(jnp.bfloat16)
        before_or_at = (row <= col).astype(jnp.float32).astype(jnp.bfloat16)
        rank = dot(start, before_or_at)[0:1].astype(jnp.int32) - 1
        slot = lax.broadcasted_iota(jnp.int32, (slots + 16, rows), 0)
        slot = jnp.where(slot >= slots, slots - 1 - slot, slot)
        onehot = (rank == slot).astype(jnp.float32)
        summed = dot(onehot.astype(jnp.bfloat16), encoded)
        counts = jnp.sum(onehot, axis=1, keepdims=True)
        sums_ref[...] = summed[0:slots]
        count_ref[...] = jnp.broadcast_to(counts[0:slots], (slots, 128))
        width = own_ref.shape[1]
        lead_ref[:, 0:width] = summed[slots : slots + 1]
        lead_ref[:, width : width + 128] = jnp.broadcast_to(counts[slots : slots + 1], (1, 128))


def far_attend(block, start_row, own, far_up, far_down, parts, w_qkv, w_out, slots):
    rows, width = own.shape
    steps = width // GROUP

    def weight(part):
        return pl.BlockSpec((width, GROUP), lambda i: (0, part * steps + i))

    def full(shape):
        return pl.BlockSpec(shape, lambda i: (0, 0))

    piece = pl.BlockSpec((rows, GROUP), lambda i: (0, i))
    return pl.pallas_call(
        far_kernel,
        grid=(steps,),
        out_shape=(
            jax.ShapeDtypeStruct((rows, width), jnp.bfloat16),
            jax.ShapeDtypeStruct((slots, width), jnp.float32),
            jax.ShapeDtypeStruct((1, width + 128), jnp.float32),
            jax.ShapeDtypeStruct((slots, 128), jnp.float32),
        ),
        in_specs=[
            pl.BlockSpec(memory_space=pltpu.SMEM),
            full((1, rows)),
            full((rows, width)),
            full(far_up.shape),
            full(far_down.shape),
            piece,
            piece,
            piece,
            piece,
            weight(1),
            weight(2),
            pl.BlockSpec((GROUP, width), lambda i: (i, 0)),
        ],
        out_specs=(full((rows, width)), full((slots, width)), full((1, width + 128)), full((slots, 128))),
        scratch_shapes=[pltpu.VMEM((rows, width), jnp.float32)],
        compiler_params=params(VMEM_ALL),
        cost_estimate=pl.CostEstimate(flops=FAR_COST, bytes_accessed=1000, transcendentals=0),
        name="far_attention",
    )(block, start_row, own, far_up, far_down, *parts, w_qkv, w_qkv, w_out)


def pool_kernel(start_ref, sums_ref, count_ref, extra_ref, out_ref):
    slots, width = sums_ref.shape
    used = jnp.sum(start_ref[...])
    last = lax.broadcasted_iota(jnp.int32, (slots, 1), 0) == used - 1
    extra = extra_ref[...]
    sums = sums_ref[...] + jnp.where(last, extra[:, 0:width], 0.0)
    count = count_ref[:, 0:1] + jnp.where(last, extra[:, width : width + 1], 0.0)
    mean = sums / jnp.maximum(count, 1.0)
    out_ref[...] = jnp.where(count > 0, mean, 0.0).astype(jnp.bfloat16)


def pool(start_row, sums, count, extra):
    return pl.pallas_call(
        pool_kernel,
        out_shape=jax.ShapeDtypeStruct(sums.shape, jnp.bfloat16),
        compiler_params=params(VMEM_SOME),
        name="patch_pool",
    )(start_row, sums, count, extra)


def local(byte_states, w_qkv, w_out, patch_start, latent_q, latent_k, latent_v):
    rows, _ = byte_states.shape
    slots = latent_q.shape[0]
    block = lax.axis_index(SEQ).astype(jnp.int32).reshape(1)
    side = lax.axis_index("yl").astype(jnp.int32).reshape(1)
    start_row = patch_start.reshape(1, rows)

    before = shift(byte_states, 1)
    relayed = down(byte_states[DOWN_FROM:], False)
    query, *parts = own_attend(byte_states, w_qkv)
    *parts, up, relayed = before_attend(block, before, relayed, (query, *parts), w_qkv)
    far_up = shift(up, 1)
    far_down = down(relayed, True)

    packed = pack(start_row, latent_q, latent_k, latent_v)
    own = lax.all_to_all(packed, ("yh", "zh"), 0, 0, tiled=True)
    other = lax.ppermute(split(own, up), "yl", [(0, 1), (1, 0)])
    heads = latent_attend(side, own, other)
    returned = lax.all_to_all(heads, ("yh", "zh"), 0, 0, tiled=True)
    latent_out = unpack(start_row, returned)

    encoded, sums, lead, count = far_attend(
        block, start_row, byte_states, far_up, far_down, (query, *parts), w_qkv, w_out, slots
    )
    extra = shift(lead, -1)
    patch_embed = pool(start_row, sums, count, extra)
    return encoded, patch_embed, latent_out


def solution(mesh):
    folded = Mesh(mesh.devices.reshape(mesh.shape["dp"], 4, 2, 4), ("dp", "yh", "yl", "zh"))
    spec = P(("dp", *SEQ), None)
    return jax.shard_map(
        local,
        mesh=folded,
        in_specs=(spec, P(), P(), P(("dp", *SEQ)), spec, spec, spec),
        out_specs=(spec, spec, spec),
        check_vma=False,
    )
```

```python
import functools

import jax
import jax.numpy as jnp
from jax import lax
from jax.experimental import pallas as pl
from jax.experimental.pallas import tpu as pltpu
from jax.sharding import Mesh, PartitionSpec as P

BYTE_HEAD = 64
LAT_HEAD = 128
GROUP = 256
NEGATIVE = -1e30
UP_ROWS = 112
MARK = 1024.0
SEQ = ("yh", "yl", "zh")
PACK_COST = 1000
OWN_COST = 30_000_000_000
BEFORE_COST = 10_000_000_000
LATENT_COST = 1000
UNPACK_COST = 1000
FAR_COST = 30_000_000_000
VMEM_ALL = 62 * 1024 * 1024
VMEM_SOME = 16 * 1024 * 1024

NT = (((1,), (1,)), ((), ()))


def shift(x, by):
    count = lax.axis_size(SEQ)
    return lax.ppermute(x, SEQ, [(i, i + by) for i in range(count) if 0 <= i + by < count])


def down(x):
    count, ring = lax.axis_size(SEQ), lax.axis_size("zh")

    def after(source, steps):
        return source - source % ring + (source - steps) % ring

    sources = range(count - 2)
    relayed = lax.ppermute(x, SEQ, [(s, after(s, 1)) for s in sources])
    return relayed, lax.ppermute(relayed, SEQ, [(after(s, 1), s + ring - 2) for s in sources])


def dot(a, b):
    return jnp.dot(a, b, preferred_element_type=jnp.float32)


def dot_nt(a, b):
    return lax.dot_general(a, b, NT, preferred_element_type=jnp.float32)


def params(limit):
    return pltpu.CompilerParams(vmem_limit_bytes=limit)


def pack_kernel(start_ref, q_ref, k_ref, v_ref, out_ref):
    used = jnp.sum(start_ref[...])
    rows = q_ref.shape[0]
    for head in range(out_ref.shape[0]):
        cols = pl.ds(head * LAT_HEAD, LAT_HEAD)
        out_ref[head, 0:rows] = q_ref[:, cols]
        slot = lax.broadcasted_iota(jnp.int32, (rows, LAT_HEAD), 0)
        key = k_ref[:, cols].astype(jnp.float32)
        out_ref[head, rows : 2 * rows] = jnp.where(slot < used, key, MARK).astype(jnp.bfloat16)
        out_ref[head, 2 * rows : 3 * rows] = v_ref[:, cols]


def pack(start_row, q, k, v):
    rows, width = q.shape
    return pl.pallas_call(
        pack_kernel,
        out_shape=jax.ShapeDtypeStruct((width // LAT_HEAD, 3 * rows, LAT_HEAD), jnp.bfloat16),
        compiler_params=params(VMEM_ALL),
        cost_estimate=pl.CostEstimate(flops=PACK_COST, bytes_accessed=1000, transcendentals=0),
        name="latent_pack",
    )(start_row, q, k, v)


def latent_kernel(side_ref, own_ref, other_ref, after_ref, out_ref):
    del after_ref
    blocks, rows3, _ = own_ref.shape
    rows = rows3 // 3
    total = blocks * rows
    side = side_ref[0]
    q = own_ref[:, 0:rows].reshape(total, LAT_HEAD)
    scale = LAT_HEAD ** (-0.5)
    pick = (lax.broadcasted_iota(jnp.int32, (16, LAT_HEAD), 1) == 0).astype(jnp.bfloat16)

    def position(index, parity):
        block = index // rows
        return ((block // 4) * 8 + parity * 4 + block % 4) * rows + index % rows

    query_pos = position(lax.broadcasted_iota(jnp.int32, (total, 1), 0), side)
    scores = []
    for which, (ref, parity) in enumerate(((own_ref, side), (other_ref, 1 - side))):
        base = rows if which == 0 else 0
        key = ref[:, base : base + rows].reshape(total, LAT_HEAD)
        mark = dot_nt(pick, key)[0:1]
        key_pos = position(lax.broadcasted_iota(jnp.int32, (1, total), 1), parity)
        key_pos = jnp.where(mark < MARK / 2, key_pos, 1 << 30)
        s = dot_nt(q, key) * scale
        scores.append(jnp.where(key_pos <= query_pos, s, NEGATIVE))
    peak = jnp.maximum(jnp.max(scores[0], axis=1, keepdims=True), jnp.max(scores[1], axis=1, keepdims=True))
    norm = jnp.zeros_like(peak)
    summed = jnp.zeros((total, LAT_HEAD), jnp.float32)
    for which, ref in enumerate((own_ref, other_ref)):
        base = 2 * rows if which == 0 else rows
        value = ref[:, base : base + rows].reshape(total, LAT_HEAD)
        weight = jnp.exp(scores[which] - peak)
        norm = norm + jnp.sum(weight, axis=1, keepdims=True)
        summed = summed + dot(weight.astype(jnp.bfloat16), value)
    out_ref[...] = (summed / norm).astype(jnp.bfloat16).reshape(blocks, rows, LAT_HEAD)


def latent_attend(side, own, other, after):
    blocks, rows3, width = own.shape
    rows = rows3 // 3
    total = blocks * rows
    return pl.pallas_call(
        latent_kernel,
        out_shape=jax.ShapeDtypeStruct((blocks, rows, width), jnp.bfloat16),
        in_specs=[
            pl.BlockSpec(memory_space=pltpu.SMEM),
            pl.BlockSpec(memory_space=pltpu.VMEM),
            pl.BlockSpec(memory_space=pltpu.VMEM),
            pl.BlockSpec(memory_space=pl.ANY),
        ],
        compiler_params=params(VMEM_SOME),
        cost_estimate=pl.CostEstimate(flops=LATENT_COST, bytes_accessed=1000, transcendentals=0),
        name="latent_attend",
    )(side, own, other, after)


def unpack_kernel(start_ref, heads_ref, out_ref):
    used = jnp.sum(start_ref[...])
    rows = out_ref.shape[0]
    for head in range(heads_ref.shape[0]):
        slot = lax.broadcasted_iota(jnp.int32, (rows, LAT_HEAD), 0)
        value = heads_ref[head].astype(jnp.float32)
        out_ref[:, pl.ds(head * LAT_HEAD, LAT_HEAD)] = jnp.where(slot < used, value, 0.0).astype(jnp.bfloat16)


def unpack(start_row, heads):
    count, rows, width = heads.shape
    return pl.pallas_call(
        unpack_kernel,
        out_shape=jax.ShapeDtypeStruct((rows, count * width), jnp.bfloat16),
        compiler_params=params(VMEM_SOME),
        cost_estimate=pl.CostEstimate(flops=UNPACK_COST, bytes_accessed=1000, transcendentals=0),
        name="latent_unpack",
    )(start_row, heads)


def halves():
    return [slice(start, start + 128) for start in range(0, GROUP, 128)]


def low_lanes(rows):
    return lax.broadcasted_iota(jnp.int32, (rows, 128), 1) < BYTE_HEAD


def split_heads(x, low, fill):
    other = jnp.full_like(x, fill)
    return jnp.where(low, x, other), jnp.where(low, other, x)


def own_kernel(own_ref, wq_ref, wk_ref, wv_ref, q_ref, acc_ref, peak_ref, norm_ref):
    rows = own_ref.shape[0]
    own = own_ref[...]
    q = dot(own, wq_ref[...]).astype(jnp.bfloat16)
    q = (q.astype(jnp.float32) * BYTE_HEAD ** (-0.5)).astype(jnp.bfloat16)
    q_ref[...] = q
    key = dot(own, wk_ref[...]).astype(jnp.bfloat16)
    value = dot(own, wv_ref[...]).astype(jnp.bfloat16)
    row = lax.broadcasted_iota(jnp.int32, (rows, rows), 0)
    col = lax.broadcasted_iota(jnp.int32, (rows, rows), 1)
    seen = col <= row
    low = low_lanes(rows)
    for half in halves():
        values = split_heads(value[:, half], low, 1.0)
        peaks, products = [], []
        for head, qh in enumerate(split_heads(q[:, half], low, 0.0)):
            s = jnp.where(seen, dot_nt(qh, key[:, half]), NEGATIVE)
            peak = jnp.max(s, axis=1, keepdims=True)
            peaks.append(peak)
            products.append(dot(jnp.exp(s - peak).astype(jnp.bfloat16), values[head]))
        acc_ref[:, half] = jnp.where(low, products[0], products[1])
        norm_ref[:, half] = pltpu.roll(jnp.where(low, products[1], products[0]), BYTE_HEAD, 1)
        peak_ref[:, half] = jnp.where(low, peaks[0], peaks[1])


def earlier_block(x, half, q_ref, acc_ref, peak_ref, norm_ref, key, value, seen):
    low = low_lanes(x)
    values = split_heads(value[:, half], low, 1.0)
    peak = peak_ref[:, half]
    peaks, products = [], []
    for head, qh in enumerate(split_heads(q_ref[:, half], low, 0.0)):
        s = jnp.where(seen, dot_nt(qh, key[:, half]), NEGATIVE)
        lane = head * BYTE_HEAD
        newer = jnp.maximum(peak[:, lane : lane + 1], jnp.max(s, axis=1, keepdims=True))
        peaks.append(newer)
        products.append(dot(jnp.exp(s - newer).astype(jnp.bfloat16), values[head]))
    newest = jnp.where(low, peaks[0], peaks[1])
    fade = jnp.exp(peak - newest)
    acc = acc_ref[:, half] * fade + jnp.where(low, products[0], products[1])
    norm = pltpu.roll(jnp.where(low, products[1], products[0]), BYTE_HEAD, 1)
    return acc, newest, norm_ref[:, half] * fade + norm


def before_kernel(
    block_ref, before_ref, q_ref, acc_ref, peak_ref, norm_ref, wk_ref, wv_ref, acc_out, peak_out, norm_out, up_out
):
    rows = before_ref.shape[0]

    @pl.when(pl.program_id(0) == 0)
    def _():
        up_out[...] = before_ref[0:UP_ROWS]

    before = before_ref[...]
    key = dot(before, wk_ref[...]).astype(jnp.bfloat16)
    value = dot(before, wv_ref[...]).astype(jnp.bfloat16)
    first = jnp.where(block_ref[0] >= 1, 0, rows)
    seen = lax.broadcasted_iota(jnp.int32, (rows, rows), 1) >= first
    for half in halves():
        acc, peak, norm = earlier_block(rows, half, q_ref, acc_ref, peak_ref, norm_ref, key, value, seen)
        acc_out[:, half] = acc
        peak_out[:, half] = peak
        norm_out[:, half] = norm


def weight_part(width, part):
    steps = width // GROUP
    return pl.BlockSpec((width, GROUP), lambda i: (0, part * steps + i))


def own_attend(own, w_qkv):
    rows, width = own.shape
    piece = pl.BlockSpec((rows, GROUP), lambda i: (0, i))
    kept = jax.ShapeDtypeStruct((rows, width), jnp.float32)
    return pl.pallas_call(
        own_kernel,
        grid=(width // GROUP,),
        out_shape=(jax.ShapeDtypeStruct((rows, width), jnp.bfloat16), kept, kept, kept),
        in_specs=[pl.BlockSpec((rows, width), lambda i: (0, 0))] + [weight_part(width, part) for part in range(3)],
        out_specs=(piece,) * 4,
        compiler_params=params(VMEM_ALL),
        cost_estimate=pl.CostEstimate(flops=OWN_COST, bytes_accessed=1000, transcendentals=0),
        name="own_attention",
    )(own, w_qkv, w_qkv, w_qkv)


def before_attend(block, before, parts, w_qkv):
    rows, width = before.shape
    piece = pl.BlockSpec((rows, GROUP), lambda i: (0, i))
    kept = jax.ShapeDtypeStruct((rows, width), jnp.float32)
    return pl.pallas_call(
        before_kernel,
        grid=(width // GROUP,),
        out_shape=(kept, kept, kept, jax.ShapeDtypeStruct((UP_ROWS, width), before.dtype)),
        in_specs=[pl.BlockSpec(memory_space=pltpu.SMEM), pl.BlockSpec((rows, width), lambda i: (0, 0))]
        + [piece] * 4
        + [weight_part(width, part) for part in (1, 2)],
        out_specs=(piece,) * 3 + (pl.BlockSpec((UP_ROWS, width), lambda i: (0, 0)),),
        compiler_params=params(VMEM_ALL),
        cost_estimate=pl.CostEstimate(flops=BEFORE_COST, bytes_accessed=1000, transcendentals=0),
        name="before_attention",
    )(block, before, *parts, w_qkv, w_qkv)


def far_kernel(
    block_ref, start_ref, own_ref, up_ref, down_ref, q_ref, acc_ref, peak_ref, norm_ref, wk_ref, wv_ref, wo_ref,
    enc_ref, sums_ref, lead_ref, count_ref, total_ref,
):
    step = pl.program_id(0)
    rows = own_ref.shape[0]
    far = jnp.concatenate([up_ref[...], down_ref[...]], axis=0)
    key = dot(far, wk_ref[...]).astype(jnp.bfloat16)
    value = dot(far, wv_ref[...]).astype(jnp.bfloat16)
    row = lax.broadcasted_iota(jnp.int32, (rows, rows), 0)
    col = lax.broadcasted_iota(jnp.int32, (rows, rows), 1)
    first = jnp.where(block_ref[0] >= 2, 0, 2 * rows)
    seen = col > row + first
    attended = []
    for half in halves():
        acc, _, norm = earlier_block(rows, half, q_ref, acc_ref, peak_ref, norm_ref, key, value, seen)
        attended.append((acc / norm).astype(jnp.bfloat16))
    attended = jnp.concatenate(attended, axis=1)
    product = dot(attended, wo_ref[...])

    @pl.when(step == 0)
    def _():
        total_ref[...] = product

    @pl.when(step > 0)
    def _():
        total_ref[...] += product

    @pl.when(step == pl.num_programs(0) - 1)
    def _():
        encoded = (own_ref[...].astype(jnp.float32) + total_ref[...]).astype(jnp.bfloat16)
        enc_ref[...] = encoded
        slots = sums_ref.shape[0]
        start = jnp.broadcast_to(start_ref[...].astype(jnp.float32), (16, rows)).astype(jnp.bfloat16)
        before_or_at = (row <= col).astype(jnp.float32).astype(jnp.bfloat16)
        rank = dot(start, before_or_at)[0:1].astype(jnp.int32) - 1
        slot = lax.broadcasted_iota(jnp.int32, (slots + 16, rows), 0)
        slot = jnp.where(slot >= slots, slots - 1 - slot, slot)
        onehot = (rank == slot).astype(jnp.float32)
        summed = dot(onehot.astype(jnp.bfloat16), encoded)
        counts = jnp.sum(onehot, axis=1, keepdims=True)
        sums_ref[...] = summed[0:slots]
        count_ref[...] = jnp.broadcast_to(counts[0:slots], (slots, 128))
        width = own_ref.shape[1]
        lead_ref[:, 0:width] = summed[slots : slots + 1]
        lead_ref[:, width : width + 128] = jnp.broadcast_to(counts[slots : slots + 1], (1, 128))


def far_attend(block, start_row, own, far_up, far_down, parts, w_qkv, w_out, slots):
    rows, width = own.shape
    steps = width // GROUP

    def weight(part):
        return pl.BlockSpec((width, GROUP), lambda i: (0, part * steps + i))

    def full(shape):
        return pl.BlockSpec(shape, lambda i: (0, 0))

    piece = pl.BlockSpec((rows, GROUP), lambda i: (0, i))
    return pl.pallas_call(
        far_kernel,
        grid=(steps,),
        out_shape=(
            jax.ShapeDtypeStruct((rows, width), jnp.bfloat16),
            jax.ShapeDtypeStruct((slots, width), jnp.float32),
            jax.ShapeDtypeStruct((1, width + 128), jnp.float32),
            jax.ShapeDtypeStruct((slots, 128), jnp.float32),
        ),
        in_specs=[
            pl.BlockSpec(memory_space=pltpu.SMEM),
            full((1, rows)),
            full((rows, width)),
            full(far_up.shape),
            full(far_down.shape),
            piece,
            piece,
            piece,
            piece,
            weight(1),
            weight(2),
            pl.BlockSpec((GROUP, width), lambda i: (i, 0)),
        ],
        out_specs=(full((rows, width)), full((slots, width)), full((1, width + 128)), full((slots, 128))),
        scratch_shapes=[pltpu.VMEM((rows, width), jnp.float32)],
        compiler_params=params(VMEM_ALL),
        cost_estimate=pl.CostEstimate(flops=FAR_COST, bytes_accessed=1000, transcendentals=0),
        name="far_attention",
    )(block, start_row, own, far_up, far_down, *parts, w_qkv, w_qkv, w_out)


def pool_kernel(start_ref, sums_ref, count_ref, extra_ref, out_ref):
    slots, width = sums_ref.shape
    used = jnp.sum(start_ref[...])
    last = lax.broadcasted_iota(jnp.int32, (slots, 1), 0) == used - 1
    extra = extra_ref[...]
    sums = sums_ref[...] + jnp.where(last, extra[:, 0:width], 0.0)
    count = count_ref[:, 0:1] + jnp.where(last, extra[:, width : width + 1], 0.0)
    mean = sums / jnp.maximum(count, 1.0)
    out_ref[...] = jnp.where(count > 0, mean, 0.0).astype(jnp.bfloat16)


def pool(start_row, sums, count, extra):
    return pl.pallas_call(
        pool_kernel,
        out_shape=jax.ShapeDtypeStruct(sums.shape, jnp.bfloat16),
        compiler_params=params(VMEM_SOME),
        name="patch_pool",
    )(start_row, sums, count, extra)


def local(byte_states, w_qkv, w_out, patch_start, latent_q, latent_k, latent_v):
    rows, _ = byte_states.shape
    slots = latent_q.shape[0]
    block = lax.axis_index(SEQ).astype(jnp.int32).reshape(1)
    side = lax.axis_index("yl").astype(jnp.int32).reshape(1)
    start_row = patch_start.reshape(1, rows)

    before = shift(byte_states, 1)
    relayed, far_down = down(byte_states[UP_ROWS:])
    query, *parts = own_attend(byte_states, w_qkv)
    *parts, up = before_attend(block, before, (query, *parts), w_qkv)
    far_up = shift(up, 1)

    packed = pack(start_row, latent_q, latent_k, latent_v)
    own = lax.all_to_all(packed, ("yh", "zh"), 0, 0, tiled=True)
    other = lax.ppermute(own[:, slots:], "yl", [(0, 1), (1, 0)])
    encoded, sums, lead, count = far_attend(
        block, start_row, byte_states, far_up, far_down, (query, *parts), w_qkv, w_out, slots
    )
    extra = shift(lead, -1)
    heads = latent_attend(side, own, other, count)
    returned = lax.all_to_all(heads, ("yh", "zh"), 0, 0, tiled=True)
    latent_out = unpack(start_row, returned)
    patch_embed = pool(start_row, sums, count, extra)
    return encoded, patch_embed, latent_out


def solution(mesh):
    folded = Mesh(mesh.devices.reshape(mesh.shape["dp"], 4, 2, 4), ("dp", "yh", "yl", "zh"))
    spec = P(("dp", *SEQ), None)
    return jax.shard_map(
        local,
        mesh=folded,
        in_specs=(spec, P(), P(), P(("dp", *SEQ)), spec, spec, spec),
        out_specs=(spec, spec, spec),
        check_vma=False,
    )
```

```python
import functools

import jax
import jax.numpy as jnp
from jax import lax
from jax.experimental import pallas as pl
from jax.experimental.pallas import tpu as pltpu
from jax.sharding import Mesh, PartitionSpec as P

BYTE_HEAD = 64
LAT_HEAD = 128
GROUP = 256
NEGATIVE = -1e30
UP_ROWS = 112
MARK = 1024.0
SEQ = ("yh", "yl", "zh")
PACK_COST = 1000
OWN_COST = 30_000_000_000
BEFORE_COST = 10_000_000_000
LATENT_COST = 1000
UNPACK_COST = 1000
FAR_COST = 30_000_000_000
VMEM_ALL = 62 * 1024 * 1024
VMEM_SOME = 16 * 1024 * 1024

NT = (((1,), (1,)), ((), ()))


def shift(x, by):
    count = lax.axis_size(SEQ)
    return lax.ppermute(x, SEQ, [(i, i + by) for i in range(count) if 0 <= i + by < count])


def down(x):
    count, ring = lax.axis_size(SEQ), lax.axis_size("zh")

    def after(source, steps):
        return source - source % ring + (source - steps) % ring

    sources = range(count - 2)
    relayed = lax.ppermute(x, SEQ, [(s, after(s, 1)) for s in sources])
    return relayed, lax.ppermute(relayed, SEQ, [(after(s, 1), s + ring - 2) for s in sources])


def dot(a, b):
    return jnp.dot(a, b, preferred_element_type=jnp.float32)


def dot_nt(a, b):
    return lax.dot_general(a, b, NT, preferred_element_type=jnp.float32)


def params(limit):
    return pltpu.CompilerParams(vmem_limit_bytes=limit)


def pack_kernel(start_ref, q_ref, k_ref, v_ref, out_ref):
    used = jnp.sum(start_ref[...])
    rows = q_ref.shape[0]
    for head in range(out_ref.shape[0]):
        cols = pl.ds(head * LAT_HEAD, LAT_HEAD)
        out_ref[head, 0:rows] = q_ref[:, cols]
        slot = lax.broadcasted_iota(jnp.int32, (rows, LAT_HEAD), 0)
        key = k_ref[:, cols].astype(jnp.float32)
        out_ref[head, rows : 2 * rows] = jnp.where(slot < used, key, MARK).astype(jnp.bfloat16)
        out_ref[head, 2 * rows : 3 * rows] = v_ref[:, cols]


def pack(start_row, q, k, v):
    rows, width = q.shape
    return pl.pallas_call(
        pack_kernel,
        out_shape=jax.ShapeDtypeStruct((width // LAT_HEAD, 3 * rows, LAT_HEAD), jnp.bfloat16),
        compiler_params=params(VMEM_ALL),
        cost_estimate=pl.CostEstimate(flops=PACK_COST, bytes_accessed=1000, transcendentals=0),
        name="latent_pack",
    )(start_row, q, k, v)


def latent_kernel(side_ref, own_ref, other_ref, out_ref):
    blocks, rows3, _ = own_ref.shape
    rows = rows3 // 3
    total = blocks * rows
    side = side_ref[0]
    q = own_ref[:, 0:rows].reshape(total, LAT_HEAD)
    scale = LAT_HEAD ** (-0.5)
    pick = (lax.broadcasted_iota(jnp.int32, (16, LAT_HEAD), 1) == 0).astype(jnp.bfloat16)

    def position(index, parity):
        block = index // rows
        return ((block // 4) * 8 + parity * 4 + block % 4) * rows + index % rows

    query_pos = position(lax.broadcasted_iota(jnp.int32, (total, 1), 0), side)
    scores = []
    for which, (ref, parity) in enumerate(((own_ref, side), (other_ref, 1 - side))):
        base = rows if which == 0 else 0
        key = ref[:, base : base + rows].reshape(total, LAT_HEAD)
        mark = dot_nt(pick, key)[0:1]
        key_pos = position(lax.broadcasted_iota(jnp.int32, (1, total), 1), parity)
        key_pos = jnp.where(mark < MARK / 2, key_pos, 1 << 30)
        s = dot_nt(q, key) * scale
        scores.append(jnp.where(key_pos <= query_pos, s, NEGATIVE))
    peak = jnp.maximum(jnp.max(scores[0], axis=1, keepdims=True), jnp.max(scores[1], axis=1, keepdims=True))
    norm = jnp.zeros_like(peak)
    summed = jnp.zeros((total, LAT_HEAD), jnp.float32)
    for which, ref in enumerate((own_ref, other_ref)):
        base = 2 * rows if which == 0 else rows
        value = ref[:, base : base + rows].reshape(total, LAT_HEAD)
        weight = jnp.exp(scores[which] - peak)
        norm = norm + jnp.sum(weight, axis=1, keepdims=True)
        summed = summed + dot(weight.astype(jnp.bfloat16), value)
    out_ref[...] = (summed / norm).astype(jnp.bfloat16).reshape(blocks, rows, LAT_HEAD)


def latent_attend(side, own, other):
    blocks, rows3, width = own.shape
    rows = rows3 // 3
    total = blocks * rows
    return pl.pallas_call(
        latent_kernel,
        out_shape=jax.ShapeDtypeStruct((blocks, rows, width), jnp.bfloat16),
        in_specs=[
            pl.BlockSpec(memory_space=pltpu.SMEM),
            pl.BlockSpec(memory_space=pltpu.VMEM),
            pl.BlockSpec(memory_space=pltpu.VMEM),
        ],
        compiler_params=params(VMEM_SOME),
        cost_estimate=pl.CostEstimate(flops=LATENT_COST, bytes_accessed=1000, transcendentals=0),
        name="latent_attend",
    )(side, own, other)


def split_kernel(own_ref, after_ref, out_ref):
    del after_ref
    rows = out_ref.shape[1] // 2
    out_ref[...] = own_ref[:, rows : 3 * rows]


def split(own, after):
    blocks, rows3, width = own.shape
    return pl.pallas_call(
        split_kernel,
        out_shape=jax.ShapeDtypeStruct((blocks, rows3 // 3 * 2, width), jnp.bfloat16),
        in_specs=[pl.BlockSpec(memory_space=pltpu.VMEM), pl.BlockSpec(memory_space=pl.ANY)],
        compiler_params=params(VMEM_SOME),
        cost_estimate=pl.CostEstimate(flops=1000, bytes_accessed=1000, transcendentals=0),
        name="latent_split",
    )(own, after)


def unpack_kernel(start_ref, heads_ref, out_ref):
    used = jnp.sum(start_ref[...])
    rows = out_ref.shape[0]
    for head in range(heads_ref.shape[0]):
        slot = lax.broadcasted_iota(jnp.int32, (rows, LAT_HEAD), 0)
        value = heads_ref[head].astype(jnp.float32)
        out_ref[:, pl.ds(head * LAT_HEAD, LAT_HEAD)] = jnp.where(slot < used, value, 0.0).astype(jnp.bfloat16)


def unpack(start_row, heads):
    count, rows, width = heads.shape
    return pl.pallas_call(
        unpack_kernel,
        out_shape=jax.ShapeDtypeStruct((rows, count * width), jnp.bfloat16),
        compiler_params=params(VMEM_SOME),
        cost_estimate=pl.CostEstimate(flops=UNPACK_COST, bytes_accessed=1000, transcendentals=0),
        name="latent_unpack",
    )(start_row, heads)


def halves():
    return [slice(start, start + 128) for start in range(0, GROUP, 128)]


def low_lanes(rows):
    return lax.broadcasted_iota(jnp.int32, (rows, 128), 1) < BYTE_HEAD


def split_heads(x, low, fill):
    other = jnp.full_like(x, fill)
    return jnp.where(low, x, other), jnp.where(low, other, x)


def own_kernel(own_ref, wq_ref, wk_ref, wv_ref, q_ref, acc_ref, peak_ref, norm_ref):
    rows = own_ref.shape[0]
    own = own_ref[...]
    q = dot(own, wq_ref[...]).astype(jnp.bfloat16)
    q = (q.astype(jnp.float32) * BYTE_HEAD ** (-0.5)).astype(jnp.bfloat16)
    q_ref[...] = q
    key = dot(own, wk_ref[...]).astype(jnp.bfloat16)
    value = dot(own, wv_ref[...]).astype(jnp.bfloat16)
    row = lax.broadcasted_iota(jnp.int32, (rows, rows), 0)
    col = lax.broadcasted_iota(jnp.int32, (rows, rows), 1)
    seen = col <= row
    low = low_lanes(rows)
    for half in halves():
        values = split_heads(value[:, half], low, 1.0)
        peaks, products = [], []
        for head, qh in enumerate(split_heads(q[:, half], low, 0.0)):
            s = jnp.where(seen, dot_nt(qh, key[:, half]), NEGATIVE)
            peak = jnp.max(s, axis=1, keepdims=True)
            peaks.append(peak)
            products.append(dot(jnp.exp(s - peak).astype(jnp.bfloat16), values[head]))
        acc_ref[:, half] = jnp.where(low, products[0], products[1])
        norm_ref[:, half] = pltpu.roll(jnp.where(low, products[1], products[0]), BYTE_HEAD, 1)
        peak_ref[:, half] = jnp.where(low, peaks[0], peaks[1])


def earlier_block(x, half, q_ref, acc_ref, peak_ref, norm_ref, key, value, seen):
    low = low_lanes(x)
    values = split_heads(value[:, half], low, 1.0)
    peak = peak_ref[:, half]
    peaks, products = [], []
    for head, qh in enumerate(split_heads(q_ref[:, half], low, 0.0)):
        s = jnp.where(seen, dot_nt(qh, key[:, half]), NEGATIVE)
        lane = head * BYTE_HEAD
        newer = jnp.maximum(peak[:, lane : lane + 1], jnp.max(s, axis=1, keepdims=True))
        peaks.append(newer)
        products.append(dot(jnp.exp(s - newer).astype(jnp.bfloat16), values[head]))
    newest = jnp.where(low, peaks[0], peaks[1])
    fade = jnp.exp(peak - newest)
    acc = acc_ref[:, half] * fade + jnp.where(low, products[0], products[1])
    norm = pltpu.roll(jnp.where(low, products[1], products[0]), BYTE_HEAD, 1)
    return acc, newest, norm_ref[:, half] * fade + norm


def before_kernel(
    block_ref, before_ref, q_ref, acc_ref, peak_ref, norm_ref, wk_ref, wv_ref, acc_out, peak_out, norm_out, up_out
):
    rows = before_ref.shape[0]

    @pl.when(pl.program_id(0) == 0)
    def _():
        up_out[...] = before_ref[0:UP_ROWS]

    before = before_ref[...]
    key = dot(before, wk_ref[...]).astype(jnp.bfloat16)
    value = dot(before, wv_ref[...]).astype(jnp.bfloat16)
    first = jnp.where(block_ref[0] >= 1, 0, rows)
    seen = lax.broadcasted_iota(jnp.int32, (rows, rows), 1) >= first
    for half in halves():
        acc, peak, norm = earlier_block(rows, half, q_ref, acc_ref, peak_ref, norm_ref, key, value, seen)
        acc_out[:, half] = acc
        peak_out[:, half] = peak
        norm_out[:, half] = norm


def weight_part(width, part):
    steps = width // GROUP
    return pl.BlockSpec((width, GROUP), lambda i: (0, part * steps + i))


def own_attend(own, w_qkv):
    rows, width = own.shape
    piece = pl.BlockSpec((rows, GROUP), lambda i: (0, i))
    kept = jax.ShapeDtypeStruct((rows, width), jnp.float32)
    return pl.pallas_call(
        own_kernel,
        grid=(width // GROUP,),
        out_shape=(jax.ShapeDtypeStruct((rows, width), jnp.bfloat16), kept, kept, kept),
        in_specs=[pl.BlockSpec((rows, width), lambda i: (0, 0))] + [weight_part(width, part) for part in range(3)],
        out_specs=(piece,) * 4,
        compiler_params=params(VMEM_ALL),
        cost_estimate=pl.CostEstimate(flops=OWN_COST, bytes_accessed=1000, transcendentals=0),
        name="own_attention",
    )(own, w_qkv, w_qkv, w_qkv)


def before_attend(block, before, parts, w_qkv):
    rows, width = before.shape
    piece = pl.BlockSpec((rows, GROUP), lambda i: (0, i))
    kept = jax.ShapeDtypeStruct((rows, width), jnp.float32)
    return pl.pallas_call(
        before_kernel,
        grid=(width // GROUP,),
        out_shape=(kept, kept, kept, jax.ShapeDtypeStruct((UP_ROWS, width), before.dtype)),
        in_specs=[pl.BlockSpec(memory_space=pltpu.SMEM), pl.BlockSpec((rows, width), lambda i: (0, 0))]
        + [piece] * 4
        + [weight_part(width, part) for part in (1, 2)],
        out_specs=(piece,) * 3 + (pl.BlockSpec((UP_ROWS, width), lambda i: (0, 0)),),
        compiler_params=params(VMEM_ALL),
        cost_estimate=pl.CostEstimate(flops=BEFORE_COST, bytes_accessed=1000, transcendentals=0),
        name="before_attention",
    )(block, before, *parts, w_qkv, w_qkv)


def far_kernel(
    block_ref, start_ref, own_ref, up_ref, down_ref, q_ref, acc_ref, peak_ref, norm_ref, wk_ref, wv_ref, wo_ref,
    enc_ref, sums_ref, lead_ref, count_ref, total_ref,
):
    step = pl.program_id(0)
    rows = own_ref.shape[0]
    far = jnp.concatenate([up_ref[...], down_ref[...]], axis=0)
    key = dot(far, wk_ref[...]).astype(jnp.bfloat16)
    value = dot(far, wv_ref[...]).astype(jnp.bfloat16)
    row = lax.broadcasted_iota(jnp.int32, (rows, rows), 0)
    col = lax.broadcasted_iota(jnp.int32, (rows, rows), 1)
    first = jnp.where(block_ref[0] >= 2, 0, 2 * rows)
    seen = col > row + first
    attended = []
    for half in halves():
        acc, _, norm = earlier_block(rows, half, q_ref, acc_ref, peak_ref, norm_ref, key, value, seen)
        attended.append((acc / norm).astype(jnp.bfloat16))
    attended = jnp.concatenate(attended, axis=1)
    product = dot(attended, wo_ref[...])

    @pl.when(step == 0)
    def _():
        total_ref[...] = product

    @pl.when(step > 0)
    def _():
        total_ref[...] += product

    @pl.when(step == pl.num_programs(0) - 1)
    def _():
        encoded = (own_ref[...].astype(jnp.float32) + total_ref[...]).astype(jnp.bfloat16)
        enc_ref[...] = encoded
        slots = sums_ref.shape[0]
        start = jnp.broadcast_to(start_ref[...].astype(jnp.float32), (16, rows)).astype(jnp.bfloat16)
        before_or_at = (row <= col).astype(jnp.float32).astype(jnp.bfloat16)
        rank = dot(start, before_or_at)[0:1].astype(jnp.int32) - 1
        slot = lax.broadcasted_iota(jnp.int32, (slots + 16, rows), 0)
        slot = jnp.where(slot >= slots, slots - 1 - slot, slot)
        onehot = (rank == slot).astype(jnp.float32)
        summed = dot(onehot.astype(jnp.bfloat16), encoded)
        counts = jnp.sum(onehot, axis=1, keepdims=True)
        sums_ref[...] = summed[0:slots]
        count_ref[...] = jnp.broadcast_to(counts[0:slots], (slots, 128))
        width = own_ref.shape[1]
        lead_ref[:, 0:width] = summed[slots : slots + 1]
        lead_ref[:, width : width + 128] = jnp.broadcast_to(counts[slots : slots + 1], (1, 128))


def far_attend(block, start_row, own, far_up, far_down, parts, w_qkv, w_out, slots):
    rows, width = own.shape
    steps = width // GROUP

    def weight(part):
        return pl.BlockSpec((width, GROUP), lambda i: (0, part * steps + i))

    def full(shape):
        return pl.BlockSpec(shape, lambda i: (0, 0))

    piece = pl.BlockSpec((rows, GROUP), lambda i: (0, i))
    return pl.pallas_call(
        far_kernel,
        grid=(steps,),
        out_shape=(
            jax.ShapeDtypeStruct((rows, width), jnp.bfloat16),
            jax.ShapeDtypeStruct((slots, width), jnp.float32),
            jax.ShapeDtypeStruct((1, width + 128), jnp.float32),
            jax.ShapeDtypeStruct((slots, 128), jnp.float32),
        ),
        in_specs=[
            pl.BlockSpec(memory_space=pltpu.SMEM),
            full((1, rows)),
            full((rows, width)),
            full(far_up.shape),
            full(far_down.shape),
            piece,
            piece,
            piece,
            piece,
            weight(1),
            weight(2),
            pl.BlockSpec((GROUP, width), lambda i: (i, 0)),
        ],
        out_specs=(full((rows, width)), full((slots, width)), full((1, width + 128)), full((slots, 128))),
        scratch_shapes=[pltpu.VMEM((rows, width), jnp.float32)],
        compiler_params=params(VMEM_ALL),
        cost_estimate=pl.CostEstimate(flops=FAR_COST, bytes_accessed=1000, transcendentals=0),
        name="far_attention",
    )(block, start_row, own, far_up, far_down, *parts, w_qkv, w_qkv, w_out)


def pool_kernel(start_ref, sums_ref, count_ref, extra_ref, after_ref, out_ref):
    del after_ref
    slots, width = sums_ref.shape
    used = jnp.sum(start_ref[...])
    last = lax.broadcasted_iota(jnp.int32, (slots, 1), 0) == used - 1
    extra = extra_ref[...]
    sums = sums_ref[...] + jnp.where(last, extra[:, 0:width], 0.0)
    count = count_ref[:, 0:1] + jnp.where(last, extra[:, width : width + 1], 0.0)
    mean = sums / jnp.maximum(count, 1.0)
    out_ref[...] = jnp.where(count > 0, mean, 0.0).astype(jnp.bfloat16)


def pool(start_row, sums, count, extra, after):
    return pl.pallas_call(
        pool_kernel,
        out_shape=jax.ShapeDtypeStruct(sums.shape, jnp.bfloat16),
        in_specs=[pl.BlockSpec(memory_space=pltpu.VMEM)] * 4 + [pl.BlockSpec(memory_space=pl.ANY)],
        compiler_params=params(VMEM_SOME),
        name="patch_pool",
    )(start_row, sums, count, extra, after)


def local(byte_states, w_qkv, w_out, patch_start, latent_q, latent_k, latent_v):
    rows, _ = byte_states.shape
    slots = latent_q.shape[0]
    block = lax.axis_index(SEQ).astype(jnp.int32).reshape(1)
    side = lax.axis_index("yl").astype(jnp.int32).reshape(1)
    start_row = patch_start.reshape(1, rows)

    before = shift(byte_states, 1)
    relayed, far_down = down(byte_states[UP_ROWS:])
    query, *parts = own_attend(byte_states, w_qkv)
    *parts, up = before_attend(block, before, (query, *parts), w_qkv)
    far_up = shift(up, 1)

    packed = pack(start_row, latent_q, latent_k, latent_v)
    own = lax.all_to_all(packed, ("yh", "zh"), 0, 0, tiled=True)
    other = lax.ppermute(split(own, up), "yl", [(0, 1), (1, 0)])
    heads = latent_attend(side, own, other)
    returned = lax.all_to_all(heads, ("yh", "zh"), 0, 0, tiled=True)
    latent_out = unpack(start_row, returned)

    encoded, sums, lead, count = far_attend(
        block, start_row, byte_states, far_up, far_down, (query, *parts), w_qkv, w_out, slots
    )
    extra = shift(lead, -1)
    patch_embed = pool(start_row, sums, count, extra, latent_out)
    return encoded, patch_embed, latent_out


def solution(mesh):
    folded = Mesh(mesh.devices.reshape(mesh.shape["dp"], 4, 2, 4), ("dp", "yh", "yl", "zh"))
    spec = P(("dp", *SEQ), None)
    return jax.shard_map(
        local,
        mesh=folded,
        in_specs=(spec, P(), P(), P(("dp", *SEQ)), spec, spec, spec),
        out_specs=(spec, spec, spec),
        check_vma=False,
    )
```

```python
import functools

import jax
import jax.numpy as jnp
from jax import lax
from jax.experimental import pallas as pl
from jax.experimental.pallas import tpu as pltpu
from jax.sharding import Mesh, PartitionSpec as P

BYTE_HEAD = 64
LAT_HEAD = 128
GROUP = 256
NEGATIVE = -1e30
UP_ROWS = 112
MARK = 1024.0
SEQ = ("yh", "yl", "zh")
PACK_COST = 1000
OWN_COST = 30_000_000_000
BEFORE_COST = 10_000_000_000
LATENT_COST = 1000
UNPACK_COST = 1000
FAR_COST = 30_000_000_000
VMEM_ALL = 62 * 1024 * 1024
VMEM_SOME = 16 * 1024 * 1024

NT = (((1,), (1,)), ((), ()))


def shift(x, by):
    count = lax.axis_size(SEQ)
    return lax.ppermute(x, SEQ, [(i, i + by) for i in range(count) if 0 <= i + by < count])


def down(x):
    count, ring = lax.axis_size(SEQ), lax.axis_size("zh")

    def after(source, steps):
        return source - source % ring + (source - steps) % ring

    sources = range(count - 2)
    relayed = lax.ppermute(x, SEQ, [(s, after(s, 1)) for s in sources])
    return relayed, lax.ppermute(relayed, SEQ, [(after(s, 1), s + ring - 2) for s in sources])


def dot(a, b):
    return jnp.dot(a, b, preferred_element_type=jnp.float32)


def dot_nt(a, b):
    return lax.dot_general(a, b, NT, preferred_element_type=jnp.float32)


def params(limit):
    return pltpu.CompilerParams(vmem_limit_bytes=limit)


def pack_kernel(start_ref, q_ref, k_ref, v_ref, out_ref):
    used = jnp.sum(start_ref[...])
    rows = q_ref.shape[0]
    for head in range(out_ref.shape[0]):
        cols = pl.ds(head * LAT_HEAD, LAT_HEAD)
        out_ref[head, 0:rows] = q_ref[:, cols]
        slot = lax.broadcasted_iota(jnp.int32, (rows, LAT_HEAD), 0)
        key = k_ref[:, cols].astype(jnp.float32)
        out_ref[head, rows : 2 * rows] = jnp.where(slot < used, key, MARK).astype(jnp.bfloat16)
        out_ref[head, 2 * rows : 3 * rows] = v_ref[:, cols]


def pack(start_row, q, k, v):
    rows, width = q.shape
    return pl.pallas_call(
        pack_kernel,
        out_shape=jax.ShapeDtypeStruct((width // LAT_HEAD, 3 * rows, LAT_HEAD), jnp.bfloat16),
        compiler_params=params(VMEM_ALL),
        cost_estimate=pl.CostEstimate(flops=PACK_COST, bytes_accessed=1000, transcendentals=0),
        name="latent_pack",
    )(start_row, q, k, v)


def latent_kernel(side_ref, own_ref, other_ref, out_ref):
    blocks, rows3, _ = own_ref.shape
    rows = rows3 // 3
    total = blocks * rows
    side = side_ref[0]
    q = own_ref[:, 0:rows].reshape(total, LAT_HEAD)
    scale = LAT_HEAD ** (-0.5)
    pick = (lax.broadcasted_iota(jnp.int32, (16, LAT_HEAD), 1) == 0).astype(jnp.bfloat16)

    def position(index, parity):
        block = index // rows
        return ((block // 4) * 8 + parity * 4 + block % 4) * rows + index % rows

    query_pos = position(lax.broadcasted_iota(jnp.int32, (total, 1), 0), side)
    scores = []
    for which, (ref, parity) in enumerate(((own_ref, side), (other_ref, 1 - side))):
        base = rows if which == 0 else 0
        key = ref[:, base : base + rows].reshape(total, LAT_HEAD)
        mark = dot_nt(pick, key)[0:1]
        key_pos = position(lax.broadcasted_iota(jnp.int32, (1, total), 1), parity)
        key_pos = jnp.where(mark < MARK / 2, key_pos, 1 << 30)
        s = dot_nt(q, key) * scale
        scores.append(jnp.where(key_pos <= query_pos, s, NEGATIVE))
    peak = jnp.maximum(jnp.max(scores[0], axis=1, keepdims=True), jnp.max(scores[1], axis=1, keepdims=True))
    norm = jnp.zeros_like(peak)
    summed = jnp.zeros((total, LAT_HEAD), jnp.float32)
    for which, ref in enumerate((own_ref, other_ref)):
        base = 2 * rows if which == 0 else rows
        value = ref[:, base : base + rows].reshape(total, LAT_HEAD)
        weight = jnp.exp(scores[which] - peak)
        norm = norm + jnp.sum(weight, axis=1, keepdims=True)
        summed = summed + dot(weight.astype(jnp.bfloat16), value)
    out_ref[...] = (summed / norm).astype(jnp.bfloat16).reshape(blocks, rows, LAT_HEAD)


def latent_attend(side, own, other):
    blocks, rows3, width = own.shape
    rows = rows3 // 3
    total = blocks * rows
    return pl.pallas_call(
        latent_kernel,
        out_shape=jax.ShapeDtypeStruct((blocks, rows, width), jnp.bfloat16),
        in_specs=[
            pl.BlockSpec(memory_space=pltpu.SMEM),
            pl.BlockSpec(memory_space=pltpu.VMEM),
            pl.BlockSpec(memory_space=pltpu.VMEM),
        ],
        compiler_params=params(VMEM_SOME),
        cost_estimate=pl.CostEstimate(flops=LATENT_COST, bytes_accessed=1000, transcendentals=0),
        name="latent_attend",
    )(side, own, other)


def split_kernel(own_ref, after_ref, out_ref):
    del after_ref
    rows = out_ref.shape[1] // 2
    out_ref[...] = own_ref[:, rows : 3 * rows]


def split(own, after):
    blocks, rows3, width = own.shape
    return pl.pallas_call(
        split_kernel,
        out_shape=jax.ShapeDtypeStruct((blocks, rows3 // 3 * 2, width), jnp.bfloat16),
        in_specs=[pl.BlockSpec(memory_space=pltpu.VMEM), pl.BlockSpec(memory_space=pl.ANY)],
        compiler_params=params(VMEM_SOME),
        cost_estimate=pl.CostEstimate(flops=1000, bytes_accessed=1000, transcendentals=0),
        name="latent_split",
    )(own, after)


def unpack_kernel(start_ref, heads_ref, out_ref):
    used = jnp.sum(start_ref[...])
    rows = out_ref.shape[0]
    for head in range(heads_ref.shape[0]):
        slot = lax.broadcasted_iota(jnp.int32, (rows, LAT_HEAD), 0)
        value = heads_ref[head].astype(jnp.float32)
        out_ref[:, pl.ds(head * LAT_HEAD, LAT_HEAD)] = jnp.where(slot < used, value, 0.0).astype(jnp.bfloat16)


def unpack(start_row, heads):
    count, rows, width = heads.shape
    return pl.pallas_call(
        unpack_kernel,
        out_shape=jax.ShapeDtypeStruct((rows, count * width), jnp.bfloat16),
        compiler_params=params(VMEM_SOME),
        cost_estimate=pl.CostEstimate(flops=UNPACK_COST, bytes_accessed=1000, transcendentals=0),
        name="latent_unpack",
    )(start_row, heads)


def halves():
    return [slice(start, start + 128) for start in range(0, GROUP, 128)]


def low_lanes(rows):
    return lax.broadcasted_iota(jnp.int32, (rows, 128), 1) < BYTE_HEAD


def split_heads(x, low, fill):
    other = jnp.full_like(x, fill)
    return jnp.where(low, x, other), jnp.where(low, other, x)


def own_kernel(own_ref, wq_ref, wk_ref, wv_ref, q_ref, acc_ref, peak_ref, norm_ref):
    rows = own_ref.shape[0]
    own = own_ref[...]
    q = dot(own, wq_ref[...]).astype(jnp.bfloat16)
    q = (q.astype(jnp.float32) * BYTE_HEAD ** (-0.5)).astype(jnp.bfloat16)
    q_ref[...] = q
    key = dot(own, wk_ref[...]).astype(jnp.bfloat16)
    value = dot(own, wv_ref[...]).astype(jnp.bfloat16)
    row = lax.broadcasted_iota(jnp.int32, (rows, rows), 0)
    col = lax.broadcasted_iota(jnp.int32, (rows, rows), 1)
    seen = col <= row
    low = low_lanes(rows)
    for half in halves():
        values = split_heads(value[:, half], low, 1.0)
        peaks, products = [], []
        for head, qh in enumerate(split_heads(q[:, half], low, 0.0)):
            s = jnp.where(seen, dot_nt(qh, key[:, half]), NEGATIVE)
            peak = jnp.max(s, axis=1, keepdims=True)
            peaks.append(peak)
            products.append(dot(jnp.exp(s - peak).astype(jnp.bfloat16), values[head]))
        acc_ref[:, half] = jnp.where(low, products[0], products[1])
        norm_ref[:, half] = pltpu.roll(jnp.where(low, products[1], products[0]), BYTE_HEAD, 1)
        peak_ref[:, half] = jnp.where(low, peaks[0], peaks[1])


def earlier_block(x, half, q_ref, acc_ref, peak_ref, norm_ref, key, value, seen):
    low = low_lanes(x)
    values = split_heads(value[:, half], low, 1.0)
    peak = peak_ref[:, half]
    peaks, products = [], []
    for head, qh in enumerate(split_heads(q_ref[:, half], low, 0.0)):
        s = jnp.where(seen, dot_nt(qh, key[:, half]), NEGATIVE)
        lane = head * BYTE_HEAD
        newer = jnp.maximum(peak[:, lane : lane + 1], jnp.max(s, axis=1, keepdims=True))
        peaks.append(newer)
        products.append(dot(jnp.exp(s - newer).astype(jnp.bfloat16), values[head]))
    newest = jnp.where(low, peaks[0], peaks[1])
    fade = jnp.exp(peak - newest)
    acc = acc_ref[:, half] * fade + jnp.where(low, products[0], products[1])
    norm = pltpu.roll(jnp.where(low, products[1], products[0]), BYTE_HEAD, 1)
    return acc, newest, norm_ref[:, half] * fade + norm


def before_kernel(
    block_ref, before_ref, q_ref, acc_ref, peak_ref, norm_ref, wk_ref, wv_ref, acc_out, peak_out, norm_out, up_out
):
    rows = before_ref.shape[0]

    @pl.when(pl.program_id(0) == 0)
    def _():
        up_out[...] = before_ref[0:UP_ROWS]

    before = before_ref[...]
    key = dot(before, wk_ref[...]).astype(jnp.bfloat16)
    value = dot(before, wv_ref[...]).astype(jnp.bfloat16)
    first = jnp.where(block_ref[0] >= 1, 0, rows)
    seen = lax.broadcasted_iota(jnp.int32, (rows, rows), 1) >= first
    for half in halves():
        acc, peak, norm = earlier_block(rows, half, q_ref, acc_ref, peak_ref, norm_ref, key, value, seen)
        acc_out[:, half] = acc
        peak_out[:, half] = peak
        norm_out[:, half] = norm


def weight_part(width, part):
    steps = width // GROUP
    return pl.BlockSpec((width, GROUP), lambda i: (0, part * steps + i))


def own_attend(own, w_qkv):
    rows, width = own.shape
    piece = pl.BlockSpec((rows, GROUP), lambda i: (0, i))
    kept = jax.ShapeDtypeStruct((rows, width), jnp.float32)
    return pl.pallas_call(
        own_kernel,
        grid=(width // GROUP,),
        out_shape=(jax.ShapeDtypeStruct((rows, width), jnp.bfloat16), kept, kept, kept),
        in_specs=[pl.BlockSpec((rows, width), lambda i: (0, 0))] + [weight_part(width, part) for part in range(3)],
        out_specs=(piece,) * 4,
        compiler_params=params(VMEM_ALL),
        cost_estimate=pl.CostEstimate(flops=OWN_COST, bytes_accessed=1000, transcendentals=0),
        name="own_attention",
    )(own, w_qkv, w_qkv, w_qkv)


def before_attend(block, before, parts, w_qkv):
    rows, width = before.shape
    piece = pl.BlockSpec((rows, GROUP), lambda i: (0, i))
    kept = jax.ShapeDtypeStruct((rows, width), jnp.float32)
    return pl.pallas_call(
        before_kernel,
        grid=(width // GROUP,),
        out_shape=(kept, kept, kept, jax.ShapeDtypeStruct((UP_ROWS, width), before.dtype)),
        in_specs=[pl.BlockSpec(memory_space=pltpu.SMEM), pl.BlockSpec((rows, width), lambda i: (0, 0))]
        + [piece] * 4
        + [weight_part(width, part) for part in (1, 2)],
        out_specs=(piece,) * 3 + (pl.BlockSpec((UP_ROWS, width), lambda i: (0, 0)),),
        compiler_params=params(VMEM_ALL),
        cost_estimate=pl.CostEstimate(flops=BEFORE_COST, bytes_accessed=1000, transcendentals=0),
        name="before_attention",
    )(block, before, *parts, w_qkv, w_qkv)


def far_kernel(
    block_ref, start_ref, own_ref, up_ref, down_ref, q_ref, acc_ref, peak_ref, norm_ref, wk_ref, wv_ref, wo_ref,
    enc_ref, sums_ref, lead_ref, total_ref,
):
    step = pl.program_id(0)
    rows = own_ref.shape[0]
    far = jnp.concatenate([up_ref[...], down_ref[...]], axis=0)
    key = dot(far, wk_ref[...]).astype(jnp.bfloat16)
    value = dot(far, wv_ref[...]).astype(jnp.bfloat16)
    row = lax.broadcasted_iota(jnp.int32, (rows, rows), 0)
    col = lax.broadcasted_iota(jnp.int32, (rows, rows), 1)
    first = jnp.where(block_ref[0] >= 2, 0, 2 * rows)
    seen = col > row + first
    attended = []
    for half in halves():
        acc, _, norm = earlier_block(rows, half, q_ref, acc_ref, peak_ref, norm_ref, key, value, seen)
        attended.append((acc / norm).astype(jnp.bfloat16))
    attended = jnp.concatenate(attended, axis=1)
    product = dot(attended, wo_ref[...])

    @pl.when(step == 0)
    def _():
        total_ref[...] = product

    @pl.when(step > 0)
    def _():
        total_ref[...] += product

    @pl.when(step == pl.num_programs(0) - 1)
    def _():
        encoded = (own_ref[...].astype(jnp.float32) + total_ref[...]).astype(jnp.bfloat16)
        enc_ref[...] = encoded
        slots = sums_ref.shape[0]
        start = jnp.broadcast_to(start_ref[...].astype(jnp.float32), (16, rows)).astype(jnp.bfloat16)
        before_or_at = (row <= col).astype(jnp.float32).astype(jnp.bfloat16)
        rank = dot(start, before_or_at)[0:1].astype(jnp.int32) - 1
        slot = lax.broadcasted_iota(jnp.int32, (slots + 16, rows), 0)
        slot = jnp.where(slot >= slots, slots - 1 - slot, slot)
        onehot = (rank == slot).astype(jnp.float32)
        summed = dot(onehot.astype(jnp.bfloat16), encoded)
        counts = jnp.sum(onehot, axis=1, keepdims=True)
        width = own_ref.shape[1]
        used = jnp.sum(start_ref[...].astype(jnp.float32), axis=1, keepdims=True)
        sums_ref[:, 0:width] = summed[0:slots]
        first_lanes = lax.broadcasted_iota(jnp.int32, (slots, 128), 1) < 64
        sums_ref[:, width : width + 128] = jnp.where(first_lanes, counts[0:slots], used)
        lead_ref[:, 0:width] = summed[slots : slots + 1]
        lead_ref[:, width : width + 128] = jnp.broadcast_to(counts[slots : slots + 1], (1, 128))


def far_attend(block, start_row, own, far_up, far_down, parts, w_qkv, w_out, slots):
    rows, width = own.shape
    steps = width // GROUP

    def weight(part):
        return pl.BlockSpec((width, GROUP), lambda i: (0, part * steps + i))

    def full(shape):
        return pl.BlockSpec(shape, lambda i: (0, 0))

    piece = pl.BlockSpec((rows, GROUP), lambda i: (0, i))
    return pl.pallas_call(
        far_kernel,
        grid=(steps,),
        out_shape=(
            jax.ShapeDtypeStruct((rows, width), jnp.bfloat16),
            jax.ShapeDtypeStruct((slots, width + 128), jnp.float32),
            jax.ShapeDtypeStruct((1, width + 128), jnp.float32),
        ),
        in_specs=[
            pl.BlockSpec(memory_space=pltpu.SMEM),
            full((1, rows)),
            full((rows, width)),
            full(far_up.shape),
            full(far_down.shape),
            piece,
            piece,
            piece,
            piece,
            weight(1),
            weight(2),
            pl.BlockSpec((GROUP, width), lambda i: (i, 0)),
        ],
        out_specs=(full((rows, width)), full((slots, width + 128)), full((1, width + 128))),
        scratch_shapes=[pltpu.VMEM((rows, width), jnp.float32)],
        compiler_params=params(VMEM_ALL),
        cost_estimate=pl.CostEstimate(flops=FAR_COST, bytes_accessed=1000, transcendentals=0),
        name="far_attention",
    )(block, start_row, own, far_up, far_down, *parts, w_qkv, w_qkv, w_out)


def pool_kernel(sums_ref, extra_ref, after_ref, out_ref):
    del after_ref
    slots, width = out_ref.shape
    used = sums_ref[:, width + 64 : width + 65].astype(jnp.int32)
    last = lax.broadcasted_iota(jnp.int32, (slots, 1), 0) == used - 1
    extra = extra_ref[...]
    sums = sums_ref[:, 0:width] + jnp.where(last, extra[:, 0:width], 0.0)
    count = sums_ref[:, width : width + 1] + jnp.where(last, extra[:, width : width + 1], 0.0)
    mean = sums / jnp.maximum(count, 1.0)
    out_ref[...] = jnp.where(count > 0, mean, 0.0).astype(jnp.bfloat16)


def pool(sums, extra, after):
    slots, spread = sums.shape
    return pl.pallas_call(
        pool_kernel,
        out_shape=jax.ShapeDtypeStruct((slots, spread - 128), jnp.bfloat16),
        in_specs=[pl.BlockSpec(memory_space=pltpu.VMEM)] * 2 + [pl.BlockSpec(memory_space=pl.ANY)],
        compiler_params=params(VMEM_SOME),
        name="patch_pool",
    )(sums, extra, after)


def local(byte_states, w_qkv, w_out, patch_start, latent_q, latent_k, latent_v):
    rows, _ = byte_states.shape
    slots = latent_q.shape[0]
    block = lax.axis_index(SEQ).astype(jnp.int32).reshape(1)
    side = lax.axis_index("yl").astype(jnp.int32).reshape(1)
    start_row = patch_start.reshape(1, rows)

    before = shift(byte_states, 1)
    relayed, far_down = down(byte_states[UP_ROWS:])
    query, *parts = own_attend(byte_states, w_qkv)
    *parts, up = before_attend(block, before, (query, *parts), w_qkv)
    far_up = shift(up, 1)

    packed = pack(start_row, latent_q, latent_k, latent_v)
    own = lax.all_to_all(packed, ("yh", "zh"), 0, 0, tiled=True)
    other = lax.ppermute(split(own, up), "yl", [(0, 1), (1, 0)])
    heads = latent_attend(side, own, other)
    returned = lax.all_to_all(heads, ("yh", "zh"), 0, 0, tiled=True)
    latent_out = unpack(start_row, returned)

    encoded, sums, lead = far_attend(
        block, start_row, byte_states, far_up, far_down, (query, *parts), w_qkv, w_out, slots
    )
    extra = shift(lead, -1)
    patch_embed = pool(sums, extra, latent_out)
    return encoded, patch_embed, latent_out


def solution(mesh):
    folded = Mesh(mesh.devices.reshape(mesh.shape["dp"], 4, 2, 4), ("dp", "yh", "yl", "zh"))
    spec = P(("dp", *SEQ), None)
    return jax.shard_map(
        local,
        mesh=folded,
        in_specs=(spec, P(), P(), P(("dp", *SEQ)), spec, spec, spec),
        out_specs=(spec, spec, spec),
        check_vma=False,
    )
```
